32 devices in a mesh: band: 8 (over z, x), comp: 2 (over y), tile: 2 (over core).
Axes of the slice: x: 2, y: 2, z: 4, core: 2. Of those that a mesh axis runs over, the one named last changes fastest.
Arguments:
- atmosphere: bfloat16 [192, 384, 768], P('band', None, ('comp', 'tile')), may hold values from -6 to 6
- spec_weight: float32 [2, 2, 2, 768, 96], P(None, None, None, ('comp', 'tile')), may hold values from -0.625 to 0.625
- spec_bias: float32 [2, 2, 2, 768], P(None, None, None, ('comp', 'tile')), may hold values from -4 to 4
- norm_gain: float32 [2, 2, 768], replicated, may hold values from 0.25 to 1.75
- norm_shift: float32 [2, 2, 768], replicated, may hold values from -3 to 3
- fc_in: bfloat16 [2, 768, 3072], P(None, None, ('comp', 'tile')), may hold values from -0.21875 to 0.21875
- fc_out: bfloat16 [2, 3072, 768], P(None, ('comp', 'tile')), may hold values from -0.109375 to 0.109375
- flux_head: bfloat16 [768, 8], P(('comp', 'tile')), may hold values from -0.21875 to 0.21875
- flux_embed: float32 [8, 256], replicated, may hold values from -2 to 2
- ocean_state: bfloat16 [384, 768, 256], P('band', ('comp', 'tile')), may hold values from -6 to 6
- sea_mask: int32 [384, 768], P('band', ('comp', 'tile')), may hold values 0 or 1
- depth_kernel: float32 [7, 7, 256], replicated, may hold values from -0.875 to 0.875
- ocean_gain: float32 [256], replicated, may hold values from 0.25 to 1.75
- ocean_shift: float32 [256], replicated, may hold values from -3 to 3
- ocean_in: bfloat16 [256, 1024], replicated, may hold values from -0.375 to 0.375
- ocean_out: bfloat16 [1024, 256], replicated, may hold values from -0.1875 to 0.1875
- layer_scale: float32 [256], replicated, may hold values from 0.3 to 1
- field_head: float32 [256, 4], replicated, may hold values from -0.375 to 0.375
- patch_embed: float32 [16, 768], P(None, ('comp', 'tile')), may hold values from -1.5 to 1.5
Outputs:
- atmosphere_next: bfloat16 [192, 384, 768], P('band', None, ('comp', 'tile'))
- ocean_next: bfloat16 [384, 768, 256], P('band', ('comp', 'tile'))
- surface_fields: float32 [384, 768, 4], P('band', ('comp', 'tile'))
The draws below stay inside these ranges and needn't reach their ends.
All inputs are finite; a program needn't handle non-finite values. No bound on the sum of `sea_mask` on one device may be relied on, other than what follows from the above.
Results may differ from the reference program's by a relative error of at most 0.0095.
Values may be sent and summed in bfloat16 or wider, within the bound.
No kernel may reach another device: no remote copies, remote signals or barrier semaphores. Data moves between devices by JAX's collectives and lax.ppermute only.
A program may use at most 192 MiB of HBM per device.

```python
import math
import jax
import jax.numpy as jnp
from jax import lax

LAT = 192
LON = 384
D = 768
FFH = 3072
OC = 256
OFF = 1024
FLUX = 8
FIELDS = 4
BS = 96
KLON = 192
OLAT = 384
OLON = 768
PATCH = 16


def touch_ends(array, rng, least, high):
    index_at = [jax.random.randint(jax.random.fold_in(rng, axis), (), 0, length) for axis, length in enumerate(array.shape)]
    longest = array.shape.index(max(array.shape))
    next_to = index_at[:longest] + [(index_at[longest] + 1) % array.shape[longest]] + index_at[longest + 1:]
    return array.at[tuple(index_at)].set(least).at[tuple(next_to)].set(high)


def block_levels(key, extent, cuts, low, largest):
    gain = 1.0
    for dim, blocks in cuts:
        heights = jax.random.uniform(jax.random.fold_in(jax.random.fold_in(key, 6), dim), (blocks,), jnp.float32, low / len(cuts), largest / len(cuts))
        gain = gain * jnp.repeat(jnp.exp(heights), extent[dim] // blocks).reshape((-1,) + (1,) * (len(extent) - 1 - dim))
    return gain


def centred(stream_key, shape, deviation, reach, split=(), dtype=jnp.bfloat16):
    drawn = jax.random.normal(stream_key, shape, jnp.float32) * deviation
    if len(split) > 0:
        drawn = block_levels(stream_key, shape, split, -0.22, 0.18) * drawn
    return jnp.clip(drawn, min=-reach, max=reach).astype(dtype)


def setup_inputs(seed: int = 0) -> dict:
    keys = jax.random.split(jax.random.key(seed), 20)
    return {
        "atmosphere": centred(keys[0], (LAT, LON, D), 1.0, 6.0, ((0, 8), (2, 4))),
        "spec_weight": centred(keys[1], (2, 2, 2, D, BS), BS ** -0.5, 0.625, ((3, 4),), jnp.float32),
        "spec_bias": centred(keys[2], (2, 2, 2, D), 0.3, 4.0, ((3, 4),), jnp.float32),
        "norm_gain": jnp.clip(1.0 + 0.15 * jax.random.normal(keys[3], (2, 2, D), jnp.float32), 0.25, 1.75),
        "norm_shift": centred(keys[4], (2, 2, D), 0.2, 3.0, (), jnp.float32),
        "fc_in": centred(keys[5], (2, D, FFH), D ** -0.5, 0.21875, ((2, 4),)),
        "fc_out": centred(keys[6], (2, FFH, D), FFH ** -0.5, 0.109375, ((1, 4),)),
        "flux_head": centred(keys[7], (D, FLUX), D ** -0.5, 0.21875, ((0, 4),)),
        "flux_embed": centred(keys[8], (FLUX, OC), FLUX ** -0.5, 2.0, (), jnp.float32),
        "ocean_state": centred(keys[9], (OLAT, OLON, OC), 1.0, 6.0, ((0, 8), (1, 4))),
        "sea_mask": touch_ends((jax.random.randint(keys[10], (OLAT, OLON), 0, 10) < 7).astype(jnp.int32), jax.random.fold_in(keys[10], 1), 0, 1),
        "depth_kernel": centred(keys[11], (7, 7, OC), 49 ** -0.5, 0.875, (), jnp.float32),
        "ocean_gain": jnp.clip(1.0 + 0.15 * jax.random.normal(keys[12], (OC,), jnp.float32), 0.25, 1.75),
        "ocean_shift": centred(keys[13], (OC,), 0.2, 3.0, (), jnp.float32),
        "ocean_in": centred(keys[14], (OC, OFF), OC ** -0.5, 0.375),
        "ocean_out": centred(keys[15], (OFF, OC), OFF ** -0.5, 0.1875),
        "layer_scale": jnp.clip(jnp.exp(jax.random.uniform(keys[16], (OC,), jnp.float32, math.log(0.3), math.log(1.0))), 0.3, 1.0),
        "field_head": centred(keys[17], (OC, FIELDS), OC ** -0.5, 0.375, (), jnp.float32),
        "patch_embed": centred(keys[18], (PATCH, D), PATCH ** -0.5, 1.5, ((1, 4),), jnp.float32),
    }


full_precision = lax.Precision.HIGHEST
eps_norm = 1e-06
shrink_level = 0.01

def layer_norm(values, scaling, offset):
    average = lax.optimization_barrier(jnp.mean(values, axis=-1, keepdims=True))
    squares = lax.optimization_barrier(jnp.mean(values * values, axis=-1, keepdims=True))
    variance = squares - average * average
    return (values - average) * lax.rsqrt(variance + eps_norm) * scaling + offset

def soft_shrink(values):
    zeros = jnp.zeros_like(values)
    return jnp.where(values > shrink_level, values - shrink_level, jnp.where(values < -shrink_level, values + shrink_level, zeros))

def group_product(values, matrix):
    return jnp.einsum('...gi,gio->...go', values, matrix, precision=full_precision)

def mix_modes(real_part, imag_part, weights, biases):
    full_shape = real_part.shape
    group_width = weights.shape[-1]
    groups = weights.shape[-2] // group_width
    real_part = real_part.reshape(full_shape[:-1] + (groups, group_width))
    imag_part = imag_part.reshape(full_shape[:-1] + (groups, group_width))
    for sublayer in range(2):
        w_real = weights[sublayer, 0].reshape(groups, group_width, group_width)
        w_imag = weights[sublayer, 1].reshape(groups, group_width, group_width)
        b_real = biases[sublayer, 0].reshape(groups, group_width)
        b_imag = biases[sublayer, 1].reshape(groups, group_width)
        new_real = group_product(real_part, w_real) - group_product(imag_part, w_imag) + b_real
        new_imag = group_product(imag_part, w_real) + group_product(real_part, w_imag) + b_imag
        if sublayer == 0:
            new_real = jnp.maximum(new_real, 0.0)
            new_imag = jnp.maximum(new_imag, 0.0)
        real_part, imag_part = (new_real, new_imag)
    return (soft_shrink(real_part).reshape(full_shape), soft_shrink(imag_part).reshape(full_shape))

def mlp_row(normed_row, w_in, w_out):
    hidden = jax.nn.gelu(jnp.dot(normed_row, w_in, preferred_element_type=jnp.float32), approximate=False).astype(jnp.bfloat16)
    return jnp.dot(hidden, w_out, preferred_element_type=jnp.float32)

def afno_block(stream, scaling, offset, weights, biases, w_in, w_out):
    values = stream.astype(jnp.float32)
    normed = layer_norm(values, scaling[0], offset[0])
    spectrum = jnp.fft.rfft(normed, axis=1, norm='ortho')[:, :KLON]
    spectrum = jnp.fft.fft(spectrum, axis=0, norm='ortho')
    real_part, imag_part = mix_modes(jnp.real(spectrum), jnp.imag(spectrum), weights, biases)
    spectrum = jnp.fft.ifft(lax.complex(real_part, imag_part), axis=0, norm='ortho')
    spectrum = jnp.pad(spectrum, ((0, 0), (0, LON // 2 + 1 - KLON), (0, 0)))
    restored = jnp.fft.irfft(spectrum, n=LON, axis=1, norm='ortho')
    after_filter = (values + restored + normed).astype(jnp.bfloat16)
    filtered = after_filter.astype(jnp.float32)
    second = layer_norm(filtered, scaling[1], offset[1]).astype(jnp.bfloat16)
    mixed = lax.map(lambda row_block: mlp_row(row_block, w_in, w_out), second)
    return (filtered + mixed).astype(jnp.bfloat16)

def reference(atmosphere, spec_weight, spec_bias, norm_gain, norm_shift, fc_in, fc_out, flux_head, flux_embed, ocean_state, sea_mask, depth_kernel, ocean_gain, ocean_shift, ocean_in, ocean_out, layer_scale, field_head, patch_embed):
    after_one = afno_block(atmosphere, norm_gain[0], norm_shift[0], spec_weight[0], spec_bias[0], fc_in[0], fc_out[0])
    fluxes = jnp.dot(after_one.reshape(-1, D), flux_head, preferred_element_type=jnp.float32).reshape(LAT, LON, FLUX)
    upsampled = jnp.repeat(jnp.repeat(fluxes, 2, axis=0), 2, axis=1)
    sea_cells = sea_mask.astype(jnp.float32)[..., None]
    forcing = jnp.einsum('ijf,fc->ijc', upsampled, flux_embed, precision=full_precision)
    start = (ocean_state.astype(jnp.float32) + sea_cells * forcing).astype(jnp.bfloat16)
    padded = jnp.pad(start.astype(jnp.float32), ((0, 0), (3, 3), (0, 0)), mode='wrap')
    padded = jnp.pad(padded, ((3, 3), (0, 0), (0, 0)))
    convolved = jnp.zeros((OLAT, OLON, OC), jnp.float32)
    for row_step in range(7):
        for col_step in range(7):
            convolved = convolved + padded[row_step:row_step + OLAT, col_step:col_step + OLON] * depth_kernel[row_step, col_step]
    normed = layer_norm(convolved, ocean_gain, ocean_shift).astype(jnp.bfloat16)
    update = lax.map(lambda row_block: mlp_row(row_block, ocean_in, ocean_out), normed)
    ocean_next = (start.astype(jnp.float32) + sea_cells * layer_scale * update).astype(jnp.bfloat16)
    surface = sea_cells * jnp.einsum('ijc,cf->ijf', ocean_next.astype(jnp.float32), field_head, precision=full_precision)
    patches = surface.reshape(LAT, 2, LON, 2, FIELDS).transpose(0, 2, 4, 1, 3).reshape(LAT, LON, PATCH)
    embedding = jnp.einsum('pqk,kd->pqd', patches, patch_embed, precision=full_precision)
    middle = (after_one.astype(jnp.float32) + embedding).astype(jnp.bfloat16)
    atmosphere_next = afno_block(middle, norm_gain[1], norm_shift[1], spec_weight[1], spec_bias[1], fc_in[1], fc_out[1])
    return (atmosphere_next, ocean_next, surface)
```

```python
import functools
import math

import jax
import jax.numpy as jnp
from jax import lax
from jax.experimental import pallas as pl
from jax.experimental.pallas import tpu as pltpu
from jax.sharding import PartitionSpec as P

full_precision = lax.Precision.HIGHEST
eps_norm = 1e-06
shrink_level = 0.01
f32 = jnp.float32
bf16 = jnp.bfloat16
quarter = ("comp", "tile")
vmem_bytes = 56 * 1024 * 1024

tail_log2 = (
    -0.9999930608094244,
    -1.1512017040487785,
    -0.45877096697476855,
    -0.053412112881497276,
    0.008080722210665518,
    -0.0007692214388919801,
    3.309301407796759e-05,
)
tail_end = 6.0


def gelu(x):
    a = jnp.minimum(jnp.abs(x), tail_end)
    power = tail_log2[-1] * a + tail_log2[-2]
    for c in tail_log2[-3::-1]:
        power = power * a + c
    return jnp.maximum(x, 0.0) - a * jnp.exp2(power)


def pick(n, cap):
    for t in range(cap, 0, -16):
        if n % t == 0:
            return t
    return n


def dot(a, b):
    return jnp.dot(a, b, preferred_element_type=f32)


def layer_norm(values, scaling, offset):
    average = jnp.mean(values, axis=-1, keepdims=True)
    squares = jnp.mean(values * values, axis=-1, keepdims=True)
    variance = squares - average * average
    return (values - average) * lax.rsqrt(variance + eps_norm) * scaling + offset


def split3(x, axis):
    high = lax.reduce_precision(x, 8, 7)
    low = x - high
    return high.astype(bf16), lax.reduce_precision(low, 8, 7).astype(bf16)


def product_left(x):
    high, low = split3(x, -1)
    return jnp.concatenate([high, low, high], axis=-1)


def product_right(x):
    high, low = split3(x, 0)
    return jnp.concatenate([high, high, low], axis=0)


def whole(shape):
    return pl.BlockSpec(shape, lambda *_: (0,) * len(shape))


def shift_sum(x, axes):
    for axis in axes:
        n = lax.axis_size(axis)
        mine = x
        for d in range(1, n):
            x = x + lax.ppermute(mine, axis, [(i, (i + d) % n) for i in range(n)])
    return x


def gathered(x, axes):
    parts = [x]
    for axis in axes:
        n = lax.axis_size(axis)
        parts = parts + [
            lax.ppermute(part, axis, [(i, (i + d) % n) for i in range(n)])
            for d in range(1, n)
            for part in parts
        ]
    return parts


def gathered_pairs(x, y, axes):
    return gathered(x, axes), gathered(y, axes)


def mlp_rows(filtered, gain, shift, w_in, w_out):
    n2 = layer_norm(filtered, gain, shift).astype(bf16)
    total = filtered
    for a, b in zip(w_in, w_out):
        total = total + dot(gelu(dot(n2, a[...])).astype(bf16), b[...])
    return total.astype(bf16)


def first_mlp_kernel(n, u_ref, gain, shift, head, *refs):
    w_in, w_out, (out_ref, flux_ref) = refs[:n], refs[n : 2 * n], refs[2 * n :]
    u = jnp.concatenate([u_ref[i].astype(f32) for i in range(u_ref.shape[0])], axis=-1)
    out = mlp_rows(u, gain[...], shift[...], w_in, w_out)
    out_ref[...] = out
    flux_ref[...] = dot(out, head[...])


def first_mlp(u, gain, shift, head, w_in, w_out):
    slots, tokens, width = u.shape
    full = slots * width
    tile = pick(tokens, 384)
    n = len(w_in)
    hidden = sum(w.shape[1] for w in w_in)
    return pl.pallas_call(
        functools.partial(first_mlp_kernel, n),
        grid=(tokens // tile,),
        in_specs=[
            pl.BlockSpec((slots, tile, width), lambda i: (0, i, 0)),
            whole((1, full)),
            whole((1, full)),
            whole(head.shape),
        ]
        + [whole(w.shape) for w in w_in]
        + [whole(w.shape) for w in w_out],
        out_specs=[
            pl.BlockSpec((tile, full), lambda i: (i, 0)),
            pl.BlockSpec((tile, head.shape[1]), lambda i: (i, 0)),
        ],
        out_shape=[
            jax.ShapeDtypeStruct((tokens, full), bf16),
            jax.ShapeDtypeStruct((tokens, head.shape[1]), f32),
        ],
        compiler_params=pltpu.CompilerParams(vmem_limit_bytes=vmem_bytes),
        cost_estimate=pl.CostEstimate(
            flops=4 * tokens * full * hidden,
            bytes_accessed=4 * tokens * full + 4 * full * hidden,
            transcendentals=tokens * hidden,
        ),
    )(u, gain, shift, head, *w_in, *w_out)


def second_mlp_kernel(n, v_ref, r_ref, gain0, shift0, gain, shift, *refs):
    w_in, w_out, out_ref = refs[:n], refs[n : 2 * n], refs[2 * n]
    v = v_ref[...].astype(f32)
    r = jnp.concatenate([r_ref[i].astype(f32) for i in range(r_ref.shape[0])], axis=-1)
    u = (v + r + layer_norm(v, gain0[...], shift0[...])).astype(bf16).astype(f32)
    out = mlp_rows(u, gain[...], shift[...], w_in, w_out)
    width = out_ref.shape[2]
    for i in range(out_ref.shape[0]):
        out_ref[i] = out[:, i * width : (i + 1) * width]


def second_mlp(v, r, gain0, shift0, gain, shift, w_in, w_out):
    slots, tokens, width = r.shape
    full = slots * width
    tile = pick(tokens, 384)
    n = len(w_in)
    hidden = sum(w.shape[1] for w in w_in)
    return pl.pallas_call(
        functools.partial(second_mlp_kernel, n),
        grid=(tokens // tile,),
        in_specs=[
            pl.BlockSpec((tile, full), lambda i: (i, 0)),
            pl.BlockSpec((slots, tile, width), lambda i: (0, i, 0)),
        ]
        + [whole((1, full))] * 4
        + [whole(w.shape) for w in w_in]
        + [whole(w.shape) for w in w_out],
        out_specs=pl.BlockSpec((slots, tile, width), lambda i: (0, i, 0)),
        out_shape=jax.ShapeDtypeStruct((slots, tokens, width), bf16),
        compiler_params=pltpu.CompilerParams(vmem_limit_bytes=vmem_bytes),
        cost_estimate=pl.CostEstimate(
            flops=4 * tokens * full * hidden,
            bytes_accessed=6 * tokens * full + 4 * full * hidden,
            transcendentals=tokens * hidden,
        ),
    )(v, r, gain0, shift0, gain, shift, *w_in, *w_out)


def middle_kernel(a_ref, p_ref, e_ref, gain, shift, v_ref, n_ref):
    v = (a_ref[...].astype(f32) + dot(p_ref[...], e_ref[...])).astype(bf16)
    v_ref[...] = v
    normed = layer_norm(v.astype(f32), gain[...], shift[...]).astype(bf16)
    width = n_ref.shape[2]
    for i in range(n_ref.shape[0]):
        n_ref[i] = normed[:, i * width : (i + 1) * width]


def make_middle(a, patches, embed, gain, shift, slots):
    tokens, full = a.shape
    tile = pick(tokens, 384)
    return pl.pallas_call(
        middle_kernel,
        grid=(tokens // tile,),
        in_specs=[
            pl.BlockSpec((tile, full), lambda i: (i, 0)),
            pl.BlockSpec((tile, patches.shape[1]), lambda i: (i, 0)),
            whole(embed.shape),
            whole((1, full)),
            whole((1, full)),
        ],
        out_specs=[
            pl.BlockSpec((tile, full), lambda i: (i, 0)),
            pl.BlockSpec((slots, tile, full // slots), lambda i: (0, i, 0)),
        ],
        out_shape=[
            jax.ShapeDtypeStruct((tokens, full), bf16),
            jax.ShapeDtypeStruct((slots, tokens, full // slots), bf16),
        ],
        compiler_params=pltpu.CompilerParams(vmem_limit_bytes=vmem_bytes),
    )(a, patches, embed, gain, shift)


def soft_shrink(y):
    return y - jnp.clip(y, -shrink_level, shrink_level)


def modes_kernel(x_ref, fwd, back, weights, biases, z_ref):
    lats = x_ref.shape[1] // 2
    for k in range(x_ref.shape[0]):
        s = dot(fwd[...], x_ref[k]).astype(bf16)
        for layer in range(2):
            s_re, s_im = s[:lats], s[lats:]
            y_re = dot(s_re, weights[layer, 0]) - dot(s_im, weights[layer, 1])
            y_im = dot(s_im, weights[layer, 0]) + dot(s_re, weights[layer, 1])
            y_re = y_re + biases[layer, 0]
            y_im = y_im + biases[layer, 1]
            if layer == 0:
                y_re, y_im = jnp.maximum(y_re, 0.0), jnp.maximum(y_im, 0.0)
            else:
                y_re, y_im = soft_shrink(y_re), soft_shrink(y_im)
            s = jnp.concatenate([y_re.astype(bf16), y_im.astype(bf16)], axis=0)
        z_ref[k] = dot(back[...], s).astype(bf16)


def mix_modes(x, fwd, back, weights, biases):
    waves, rows, width = x.shape
    step = 3 if waves % 3 == 0 else 1
    return pl.pallas_call(
        modes_kernel,
        grid=(waves // step,),
        in_specs=[
            pl.BlockSpec((step, rows, width), lambda i: (i, 0, 0)),
            whole(fwd.shape),
            whole(back.shape),
            whole(weights.shape),
            whole(biases.shape),
        ],
        out_specs=pl.BlockSpec((step, rows, width), lambda i: (i, 0, 0)),
        out_shape=jax.ShapeDtypeStruct(x.shape, bf16),
        compiler_params=pltpu.CompilerParams(vmem_limit_bytes=vmem_bytes),
        cost_estimate=pl.CostEstimate(
            flops=waves * 4 * (rows * rows * width + 2 * rows * width * width),
            bytes_accessed=4 * waves * rows * width,
            transcendentals=0,
        ),
    )(x, fwd, back, weights, biases)


def ocean_kernel(on_ref, start_ref, mask_ref, w_in, w_out, scale, head, next_ref, field_ref):
    half = w_in.shape[1] // 2
    fields = field_ref.shape[1]
    total = None
    for i in range(2):
        h = gelu(dot(on_ref[...], w_in[:, i * half : (i + 1) * half])).astype(bf16)
        part = dot(h, w_out[i * half : (i + 1) * half, :])
        total = part if total is None else total + part
    mask = mask_ref[...]
    out = (start_ref[...].astype(f32) + mask * (scale[...] * total)).astype(bf16)
    next_ref[...] = out
    parts = dot(out, head[...])
    field_ref[...] = mask * (
        parts[:, :fields] + parts[:, fields : 2 * fields] + parts[:, 2 * fields :]
    )


def ocean_mlp(on, start, mask, w_in, w_out, scale, head):
    cells, width = on.shape
    tile = pick(cells, 768)
    fields = head.shape[1]
    high = lax.reduce_precision(head, 8, 7)
    mid = lax.reduce_precision(head - high, 8, 7)
    heads = jnp.concatenate([high, mid, head - high - mid], axis=1).astype(bf16)
    rows = lambda n: pl.BlockSpec((tile, n), lambda i: (i, 0))
    return pl.pallas_call(
        ocean_kernel,
        grid=(cells // tile,),
        in_specs=[
            rows(width),
            rows(width),
            rows(1),
            whole(w_in.shape),
            whole(w_out.shape),
            whole((1, width)),
            whole(heads.shape),
        ],
        out_specs=[rows(width), rows(fields)],
        out_shape=[
            jax.ShapeDtypeStruct((cells, width), bf16),
            jax.ShapeDtypeStruct((cells, fields), f32),
        ],
        compiler_params=pltpu.CompilerParams(vmem_limit_bytes=vmem_bytes),
        cost_estimate=pl.CostEstimate(
            flops=4 * cells * width * w_in.shape[1],
            bytes_accessed=8 * cells * width,
            transcendentals=cells * w_in.shape[1],
        ),
    )(on, start, mask, w_in, w_out, scale[None], heads)


def phases(count_first, count_second, length):
    first_index = lax.broadcasted_iota(jnp.int32, (count_first, count_second), 0)
    second_index = lax.broadcasted_iota(jnp.int32, (count_first, count_second), 1)
    turns = first_index * second_index % length
    return turns.astype(f32) * (2.0 * math.pi / length)


def lon_matrices(longitudes, bands):
    kept = longitudes // 2
    scale = 1.0 / math.sqrt(longitudes)
    angles = phases(longitudes, kept, longitudes)
    cos, sin = jnp.cos(angles) * scale, jnp.sin(angles) * scale
    weight = jnp.where(lax.broadcasted_iota(jnp.int32, (1, kept), 1) == 0, 1.0, 2.0)
    shape = (longitudes, bands, kept // bands, 1)

    def laid(re, im):
        both = jnp.concatenate([re.reshape(shape), im.reshape(shape)], axis=-1)
        return both.reshape(longitudes, -1).astype(bf16)

    return laid(cos, -sin), laid(cos * weight, -sin * weight)


def lat_matrices(lats):
    angles = phases(lats, lats, lats)
    cos = jnp.cos(angles) / math.sqrt(lats)
    sin = jnp.sin(angles) / math.sqrt(lats)
    fwd = jnp.concatenate(
        [jnp.concatenate([cos, sin], axis=1), jnp.concatenate([-sin, cos], axis=1)], axis=0
    )
    back = jnp.concatenate(
        [jnp.concatenate([cos, -sin], axis=1), jnp.concatenate([sin, cos], axis=1)], axis=0
    )
    return fwd.astype(bf16), back.astype(bf16)


def dense_groups(weights):
    width, group = weights.shape[-2], weights.shape[-1]
    groups = width // group
    tiled = jnp.concatenate([weights] * groups, axis=-1)
    row = lax.broadcasted_iota(jnp.int32, (width, width), 0) // group
    column = lax.broadcasted_iota(jnp.int32, (width, width), 1) // group
    return jnp.where(row == column, tiled, 0.0).astype(bf16)


def spectral_filter(normed, lon_fwd, lon_back, lat_fwd, lat_back, weights, biases):
    rows, longitudes, width = normed.shape
    bands = lax.axis_size("band")
    waves = longitudes // 2 // bands
    lats = rows * bands
    x = jnp.einsum("lnc,nx->xlc", normed, lon_fwd, preferred_element_type=f32).astype(bf16)
    x = lax.all_to_all(
        x.reshape(bands, waves, 2, rows, width), "band", split_axis=0, concat_axis=0, tiled=True
    )
    x = x.transpose(1, 2, 0, 3, 4).reshape(waves, 2 * lats, width)
    z = mix_modes(x, lat_fwd, lat_back, weights, biases)
    z = z.reshape(waves, 2, bands, rows, width).transpose(2, 0, 1, 3, 4)
    z = lax.all_to_all(z, "band", split_axis=0, concat_axis=0, tiled=True)
    z = z.reshape(bands * waves * 2, rows, width)
    return jnp.einsum("xlc,nx->lnc", z, lon_back, preferred_element_type=f32)


def with_halo(cells, sides, width, closed):
    for axis, dim in sides:
        count = lax.axis_size(axis)
        ends = count if closed else count - 1
        head = lax.slice_in_dim(cells, 0, width, axis=dim)
        tail = lax.slice_in_dim(cells, cells.shape[dim] - width, cells.shape[dim], axis=dim)
        cells = jnp.concatenate(
            [
                lax.ppermute(tail, axis, [(i, (i + 1) % count) for i in range(ends)]),
                cells,
                lax.ppermute(head, axis, [((i + 1) % count, i) for i in range(ends)]),
            ],
            axis=dim,
        )
    return cells


def on_device(
    atmosphere,
    spec_weight,
    spec_bias,
    norm_gain,
    norm_shift,
    fc_in,
    fc_out,
    flux_head,
    flux_embed,
    ocean_state,
    sea_mask,
    depth_kernel,
    ocean_gain,
    ocean_shift,
    ocean_in,
    ocean_out,
    layer_scale,
    field_head,
    patch_embed,
):
    column_index = lax.axis_index(quarter)
    slots = lax.axis_size(quarter)
    bands = lax.axis_size("band")
    rows, longitudes, slot = atmosphere.shape
    width_full = slot * slots
    part = longitudes // slots
    lon_fwd, lon_back = lon_matrices(longitudes, bands)
    lat_fwd, lat_back = lat_matrices(rows * bands)
    weights = dense_groups(spec_weight)
    biases = spec_bias[:, :, :, None, :]
    heads = lax.all_gather(flux_head, quarter, axis=0, tiled=True)
    embed = lax.all_gather(patch_embed, quarter, axis=1, tiled=True)
    gain = lambda b, i: norm_gain[b, i][None]
    shift = lambda b, i: norm_shift[b, i][None]

    values = atmosphere.astype(f32)
    sums = jnp.stack([jnp.sum(values, axis=-1), jnp.sum(values * values, axis=-1)])
    sums = shift_sum(sums, ("tile", "comp")) / width_full
    average = sums[0][..., None]
    variance = sums[1][..., None] - average * average
    scaling = lax.dynamic_slice_in_dim(norm_gain[0, 0], column_index * slot, slot)
    offset = lax.dynamic_slice_in_dim(norm_shift[0, 0], column_index * slot, slot)
    normed = (values - average) * lax.rsqrt(variance + eps_norm) * scaling + offset
    restored = spectral_filter(
        normed.astype(bf16), lon_fwd, lon_back, lat_fwd, lat_back, weights[0], biases[0]
    )
    u = (values + restored + normed).astype(bf16)
    u = u.reshape(rows, slots, part, slot).transpose(1, 0, 2, 3)
    u = lax.all_to_all(u, quarter, split_axis=0, concat_axis=0, tiled=True)
    w_in, w_out = gathered_pairs(fc_in[0], fc_out[0], ("comp", "tile"))
    after_one, fluxes = first_mlp(
        u.reshape(slots, rows * part, slot), gain(0, 1), shift(0, 1), heads, w_in, w_out
    )

    upsampled = jnp.repeat(jnp.repeat(fluxes.reshape(rows, part, -1), 2, axis=0), 2, axis=1)
    sea_cells = sea_mask.astype(f32)[..., None]
    forcing = jnp.einsum("ijf,fc->ijc", upsampled, flux_embed, precision=full_precision)
    start = (ocean_state.astype(f32) + sea_cells * forcing).astype(bf16)
    widened = with_halo(start, ((quarter, 1),), 3, True)
    extended = with_halo(widened, (("band", 0),), 3, False).astype(f32)
    tile_rows = start.shape[0]
    tile_columns = start.shape[1]
    convolved = jnp.zeros(start.shape, f32)
    for row_step in range(7):
        for col_step in range(7):
            convolved = (
                convolved
                + extended[row_step : row_step + tile_rows, col_step : col_step + tile_columns]
                * depth_kernel[row_step, col_step]
            )
    normed = layer_norm(convolved, ocean_gain, ocean_shift).astype(bf16)
    cells = tile_rows * tile_columns
    ocean_next, surface = ocean_mlp(
        normed.reshape(cells, -1),
        start.reshape(cells, -1),
        sea_cells.reshape(cells, 1),
        ocean_in,
        ocean_out,
        layer_scale,
        field_head,
    )
    ocean_next = ocean_next.reshape(start.shape)
    surface = surface.reshape(tile_rows, tile_columns, -1)

    patches = (
        surface.reshape(rows, 2, part, 2, surface.shape[2])
        .transpose(0, 2, 4, 1, 3)
        .reshape(rows * part, -1)
    )
    middle, normed = make_middle(
        after_one,
        product_left(patches),
        product_right(embed),
        gain(1, 0),
        shift(1, 0),
        slots,
    )
    normed = lax.all_to_all(normed, quarter, split_axis=0, concat_axis=0, tiled=True)
    normed = normed.reshape(slots, rows, part, slot).transpose(1, 0, 2, 3)
    restored = spectral_filter(
        normed.reshape(rows, longitudes, slot),
        lon_fwd,
        lon_back,
        lat_fwd,
        lat_back,
        weights[1],
        biases[1],
    ).astype(bf16)
    restored = restored.reshape(rows, slots, part, slot).transpose(1, 0, 2, 3)
    restored = lax.all_to_all(restored, quarter, split_axis=0, concat_axis=0, tiled=True)
    w_in, w_out = gathered_pairs(fc_in[1], fc_out[1], ("comp", "tile"))
    out = second_mlp(
        middle,
        restored.reshape(slots, rows * part, slot),
        gain(1, 0),
        shift(1, 0),
        gain(1, 1),
        shift(1, 1),
        w_in,
        w_out,
    )
    out = lax.all_to_all(out, quarter, split_axis=0, concat_axis=0, tiled=True)
    out = out.reshape(slots, rows, part, slot).transpose(1, 0, 2, 3)
    return (out.reshape(rows, longitudes, slot), ocean_next, surface)


def solution(mesh):
    placed = (
        P("band", None, ("comp", "tile")),
        P(None, None, None, ("comp", "tile"), None),
        P(None, None, None, ("comp", "tile")),
        P(),
        P(),
        P(None, None, ("comp", "tile")),
        P(None, ("comp", "tile"), None),
        P(("comp", "tile"), None),
        P(),
        P("band", ("comp", "tile"), None),
        P("band", ("comp", "tile")),
        P(),
        P(),
        P(),
        P(),
        P(),
        P(),
        P(),
        P(None, ("comp", "tile")),
    )
    return jax.shard_map(
        on_device,
        mesh=mesh,
        in_specs=placed,
        out_specs=(
            P("band", None, ("comp", "tile")),
            P("band", ("comp", "tile"), None),
            P("band", ("comp", "tile"), None),
        ),
        check_vma=False,
    )
```

```python
import functools
import math

import jax
import jax.numpy as jnp
from jax import lax
from jax.experimental import pallas as pl
from jax.experimental.pallas import tpu as pltpu
from jax.sharding import PartitionSpec as P

full_precision = lax.Precision.HIGHEST
eps_norm = 1e-06
shrink_level = 0.01
f32 = jnp.float32
bf16 = jnp.bfloat16
quarter = ("comp", "tile")
vmem_bytes = 56 * 1024 * 1024

tail_log2 = (
    -0.9999930608094244,
    -1.1512017040487785,
    -0.45877096697476855,
    -0.053412112881497276,
    0.008080722210665518,
    -0.0007692214388919801,
    3.309301407796759e-05,
)
tail_end = 6.0


def gelu(x):
    a = jnp.minimum(jnp.abs(x), tail_end)
    power = tail_log2[-1] * a + tail_log2[-2]
    for c in tail_log2[-3::-1]:
        power = power * a + c
    return jnp.maximum(x, 0.0) - a * jnp.exp2(power)


def pick(n, cap):
    for t in range(cap, 0, -16):
        if n % t == 0:
            return t
    return n


def dot(a, b):
    return jnp.dot(a, b, preferred_element_type=f32)


def layer_norm(values, scaling, offset):
    average = jnp.mean(values, axis=-1, keepdims=True)
    squares = jnp.mean(values * values, axis=-1, keepdims=True)
    variance = squares - average * average
    return (values - average) * lax.rsqrt(variance + eps_norm) * scaling + offset


def split3(x, axis):
    high = lax.reduce_precision(x, 8, 7)
    low = x - high
    return high.astype(bf16), lax.reduce_precision(low, 8, 7).astype(bf16)


def product_left(x):
    high, low = split3(x, -1)
    return jnp.concatenate([high, low, high], axis=-1)


def product_right(x):
    high, low = split3(x, 0)
    return jnp.concatenate([high, high, low], axis=0)


def whole(shape):
    return pl.BlockSpec(shape, lambda *_: (0,) * len(shape))


def shift_sum(x, axes):
    for axis in axes:
        n = lax.axis_size(axis)
        mine = x
        for d in range(1, n):
            x = x + lax.ppermute(mine, axis, [(i, (i + d) % n) for i in range(n)])
    return x


def gathered(x, axes):
    parts = [x]
    for axis in axes:
        n = lax.axis_size(axis)
        parts = parts + [
            lax.ppermute(part, axis, [(i, (i + d) % n) for i in range(n)])
            for d in range(1, n)
            for part in parts
        ]
    return parts


def gathered_pairs(x, y, axes):
    return gathered(x, axes), gathered(y, axes)


def mlp_rows(filtered, gain, shift, w_in, w_out):
    n2 = layer_norm(filtered, gain, shift).astype(bf16)
    total = filtered
    for a, b in zip(w_in, w_out):
        total = total + dot(gelu(dot(n2, a[...])).astype(bf16), b[...])
    return total.astype(bf16)


def first_mlp_kernel(n, u_ref, gain, shift, head, *refs):
    w_in, w_out, (out_ref, flux_ref) = refs[:n], refs[n : 2 * n], refs[2 * n :]
    u = jnp.concatenate([u_ref[i].astype(f32) for i in range(u_ref.shape[0])], axis=-1)
    out = mlp_rows(u, gain[...], shift[...], w_in, w_out)
    out_ref[...] = out
    flux_ref[...] = dot(out, head[...])


def first_mlp(u, gain, shift, head, w_in, w_out):
    slots, tokens, width = u.shape
    full = slots * width
    tile = pick(tokens, 384)
    n = len(w_in)
    hidden = sum(w.shape[1] for w in w_in)
    return pl.pallas_call(
        functools.partial(first_mlp_kernel, n),
        grid=(tokens // tile,),
        in_specs=[
            pl.BlockSpec((slots, tile, width), lambda i: (0, i, 0)),
            whole((1, full)),
            whole((1, full)),
            whole(head.shape),
        ]
        + [whole(w.shape) for w in w_in]
        + [whole(w.shape) for w in w_out],
        out_specs=[
            pl.BlockSpec((tile, full), lambda i: (i, 0)),
            pl.BlockSpec((tile, head.shape[1]), lambda i: (i, 0)),
        ],
        out_shape=[
            jax.ShapeDtypeStruct((tokens, full), bf16),
            jax.ShapeDtypeStruct((tokens, head.shape[1]), f32),
        ],
        compiler_params=pltpu.CompilerParams(vmem_limit_bytes=vmem_bytes),
        cost_estimate=pl.CostEstimate(
            flops=4 * tokens * full * hidden,
            bytes_accessed=4 * tokens * full + 4 * full * hidden,
            transcendentals=tokens * hidden,
        ),
    )(u, gain, shift, head, *w_in, *w_out)


def second_mlp_kernel(n, v_ref, r_ref, gain0, shift0, gain, shift, *refs):
    w_in, w_out, out_ref = refs[:n], refs[n : 2 * n], refs[2 * n]
    v = v_ref[...].astype(f32)
    r = jnp.concatenate([r_ref[i].astype(f32) for i in range(r_ref.shape[0])], axis=-1)
    u = (v + r + layer_norm(v, gain0[...], shift0[...])).astype(bf16).astype(f32)
    out = mlp_rows(u, gain[...], shift[...], w_in, w_out)
    width = out_ref.shape[2]
    for i in range(out_ref.shape[0]):
        out_ref[i] = out[:, i * width : (i + 1) * width]


def second_mlp(v, r, gain0, shift0, gain, shift, w_in, w_out):
    slots, tokens, width = r.shape
    full = slots * width
    tile = pick(tokens, 384)
    n = len(w_in)
    hidden = sum(w.shape[1] for w in w_in)
    return pl.pallas_call(
        functools.partial(second_mlp_kernel, n),
        grid=(tokens // tile,),
        in_specs=[
            pl.BlockSpec((tile, full), lambda i: (i, 0)),
            pl.BlockSpec((slots, tile, width), lambda i: (0, i, 0)),
        ]
        + [whole((1, full))] * 4
        + [whole(w.shape) for w in w_in]
        + [whole(w.shape) for w in w_out],
        out_specs=pl.BlockSpec((slots, tile, width), lambda i: (0, i, 0)),
        out_shape=jax.ShapeDtypeStruct((slots, tokens, width), bf16),
        compiler_params=pltpu.CompilerParams(vmem_limit_bytes=vmem_bytes),
        cost_estimate=pl.CostEstimate(
            flops=4 * tokens * full * hidden,
            bytes_accessed=6 * tokens * full + 4 * full * hidden,
            transcendentals=tokens * hidden,
        ),
    )(v, r, gain0, shift0, gain, shift, *w_in, *w_out)


def middle_kernel(a_ref, p_ref, e_ref, gain, shift, v_ref, n_ref):
    v = (a_ref[...].astype(f32) + dot(p_ref[...], e_ref[...])).astype(bf16)
    v_ref[...] = v
    normed = layer_norm(v.astype(f32), gain[...], shift[...]).astype(bf16)
    width = n_ref.shape[2]
    for i in range(n_ref.shape[0]):
        n_ref[i] = normed[:, i * width : (i + 1) * width]


def make_middle(a, patches, embed, gain, shift, slots):
    tokens, full = a.shape
    tile = pick(tokens, 384)
    return pl.pallas_call(
        middle_kernel,
        grid=(tokens // tile,),
        in_specs=[
            pl.BlockSpec((tile, full), lambda i: (i, 0)),
            pl.BlockSpec((tile, patches.shape[1]), lambda i: (i, 0)),
            whole(embed.shape),
            whole((1, full)),
            whole((1, full)),
        ],
        out_specs=[
            pl.BlockSpec((tile, full), lambda i: (i, 0)),
            pl.BlockSpec((slots, tile, full // slots), lambda i: (0, i, 0)),
        ],
        out_shape=[
            jax.ShapeDtypeStruct((tokens, full), bf16),
            jax.ShapeDtypeStruct((slots, tokens, full // slots), bf16),
        ],
        compiler_params=pltpu.CompilerParams(vmem_limit_bytes=vmem_bytes),
    )(a, patches, embed, gain, shift)


def soft_shrink(y):
    return y - jnp.clip(y, -shrink_level, shrink_level)


def modes_kernel(halves, pair, x_refs, fwd, back, weights, biases, z_refs):
    width = weights.shape[2]
    waves = z_refs[0].shape[0]
    for k in range(waves):
        x = jnp.concatenate(
            [
                x_refs[h][2 * k + part, :, j * width : (j + 1) * width]
                for part in range(2)
                for h in range(halves)
                for j in range(pair)
            ],
            axis=0,
        )
        lats = x.shape[0] // 2
        s = dot(fwd[...], x).astype(bf16)
        for layer in range(2):
            s_re, s_im = s[:lats], s[lats:]
            y_re = dot(s_re, weights[layer, 0]) - dot(s_im, weights[layer, 1])
            y_im = dot(s_im, weights[layer, 0]) + dot(s_re, weights[layer, 1])
            y_re = y_re + biases[layer, 0]
            y_im = y_im + biases[layer, 1]
            if layer == 0:
                y_re, y_im = jnp.maximum(y_re, 0.0), jnp.maximum(y_im, 0.0)
            else:
                y_re, y_im = soft_shrink(y_re), soft_shrink(y_im)
            s = jnp.concatenate([y_re.astype(bf16), y_im.astype(bf16)], axis=0)
        z = dot(back[...], s)
        rows = z.shape[0] // (halves * pair)
        for h in range(halves):
            cut = [z[(h * pair + j) * rows : (h * pair + j + 1) * rows] for j in range(pair)]
            z_refs[h][k] = jnp.concatenate(cut, axis=-1).astype(bf16)


def mix_modes(xs, fwd, back, weights, biases, pair, early):
    halves = len(xs)
    parts, rows, lanes = xs[0].shape
    waves = parts // 2
    lats = fwd.shape[0] // 2
    width = lanes // pair
    step = 3 if waves % 3 == 0 else 1

    def kernel(*refs):
        x_refs, refs = refs[:halves], refs[halves:]
        z_refs = refs[4 + len(early) :]
        modes_kernel(halves, pair, x_refs, *refs[:4], z_refs)

    return pl.pallas_call(
        kernel,
        grid=(waves // step,),
        in_specs=[pl.BlockSpec((2 * step, rows, lanes), lambda i: (i, 0, 0))] * halves
        + [whole(fwd.shape), whole(back.shape), whole(weights.shape), whole(biases.shape)]
        + [pl.BlockSpec(memory_space=pl.ANY)] * len(early),
        out_specs=[pl.BlockSpec((step, 2 * rows, lanes), lambda i: (i, 0, 0))] * halves,
        out_shape=[jax.ShapeDtypeStruct((waves, 2 * rows, lanes), bf16)] * halves,
        compiler_params=pltpu.CompilerParams(vmem_limit_bytes=vmem_bytes),
        cost_estimate=pl.CostEstimate(
            flops=waves * 16 * (lats * lats * width + lats * width * width),
            bytes_accessed=8 * waves * lats * width,
            transcendentals=0,
        ),
    )(*xs, fwd, back, weights, biases, *early)


def norm_with(values, stats, scaling, offset):
    column = jnp.transpose(stats)
    return (values - column[:, 0:1]) * column[:, 1:2] * scaling + offset


def aligned(waves):
    return 2 * waves % 16 == 0


def spectrum_block(bands, waves, lanes):
    if aligned(waves):
        return pl.BlockSpec((bands, 1, 2 * waves, lanes), lambda i: (0, i, 0, 0))
    return pl.BlockSpec((1, bands * 2 * waves, lanes), lambda i: (i, 0, 0))


def lon_forward(source, matrix, bands, waves, pair, stats=None):
    if stats is None:
        _, rows, part, width = source.shape
    else:
        rows, longitudes, width = source.shape
    lanes = pair * width

    def kernel(*refs):
        x_ref, f_ref, out_ref = refs[0], refs[1], refs[-1]
        columns = []
        for j in range(pair):
            if stats is None:
                columns.append(
                    jnp.concatenate([x_ref[i, j] for i in range(x_ref.shape[0])], axis=0)
                )
            else:
                st_ref, gain, shift = refs[2:5]
                normed = norm_with(x_ref[j].astype(f32), st_ref[j], gain[...], shift[...])
                columns.append(normed.astype(bf16))
        y = dot(f_ref[...], jnp.concatenate(columns, axis=-1)).astype(bf16)
        if aligned(waves):
            out_ref[:, 0] = y.reshape(bands, 2 * waves, lanes)
        else:
            out_ref[0] = y

    if stats is None:
        args = (source, matrix)
        specs = [
            pl.BlockSpec((source.shape[0], pair, part, width), lambda i: (0, i, 0, 0)),
            whole(matrix.shape),
        ]
    else:
        st, gain, shift = stats
        args = (source, matrix, st, gain, shift)
        specs = [
            pl.BlockSpec((pair, longitudes, width), lambda i: (i, 0, 0)),
            whole(matrix.shape),
            pl.BlockSpec((pair, st.shape[1], longitudes), lambda i: (i, 0, 0)),
            whole(gain.shape),
            whole(shift.shape),
        ]
    count = rows // pair
    if aligned(waves):
        shape = (bands, count, 2 * waves, lanes)
    else:
        shape = (count, bands * 2 * waves, lanes)
    out = pl.pallas_call(
        kernel,
        grid=(count,),
        in_specs=specs,
        out_specs=spectrum_block(bands, waves, lanes),
        out_shape=jax.ShapeDtypeStruct(shape, bf16),
        compiler_params=pltpu.CompilerParams(vmem_limit_bytes=vmem_bytes),
        cost_estimate=pl.CostEstimate(
            flops=2 * rows * matrix.shape[0] * matrix.shape[1] * width,
            bytes_accessed=4 * rows * matrix.shape[0] * width,
            transcendentals=0,
        ),
    )(*args)
    if not aligned(waves):
        out = out.reshape(count, bands, 2 * waves, lanes).transpose(1, 0, 2, 3)
    return out


def lon_back_call(z, matrix, slots, pair, source=None, stats=None, early=()):
    bands, count, parts, lanes = z.shape
    waves = parts // 2
    width = lanes // pair
    longitudes = matrix.shape[0]
    part = longitudes // slots
    if not aligned(waves):
        z = z.transpose(1, 0, 2, 3).reshape(count, bands * parts, lanes)

    def kernel(*refs):
        z_ref, g_ref, out_ref = refs[0], refs[1], refs[-1]
        spectra = z_ref[:, 0].reshape(bands * parts, lanes) if aligned(waves) else z_ref[0]
        r = dot(g_ref[...], spectra)
        for j in range(pair):
            u = r[:, j * width : (j + 1) * width]
            if stats is not None:
                v_ref, st_ref, gain, shift = refs[2:6]
                v = v_ref[j].astype(f32)
                u = v + u + norm_with(v, st_ref[j], gain[...], shift[...])
            u = u.astype(bf16)
            for i in range(slots):
                out_ref[i, j] = u[i * part : (i + 1) * part]

    args = [z, matrix]
    specs = [spectrum_block(bands, waves, lanes), whole(matrix.shape)]
    if stats is not None:
        st, gain, shift = stats
        args += [source, st, gain, shift]
        specs += [
            pl.BlockSpec((pair, longitudes, width), lambda i: (i, 0, 0)),
            pl.BlockSpec((pair, st.shape[1], longitudes), lambda i: (i, 0, 0)),
            whole(gain.shape),
            whole(shift.shape),
        ]
    return pl.pallas_call(
        kernel,
        grid=(count,),
        in_specs=specs + [pl.BlockSpec(memory_space=pl.ANY)] * len(early),
        out_specs=pl.BlockSpec((slots, pair, part, width), lambda i: (0, i, 0, 0)),
        out_shape=jax.ShapeDtypeStruct((slots, count * pair, part, width), bf16),
        compiler_params=pltpu.CompilerParams(vmem_limit_bytes=vmem_bytes),
        cost_estimate=pl.CostEstimate(
            flops=2 * count * longitudes * bands * parts * lanes,
            bytes_accessed=6 * count * longitudes * lanes,
            transcendentals=0,
        ),
    )(*args, *early)


def assemble_kernel(halves, *refs):
    out_ref = refs[halves]
    rows = refs[0].shape[1]
    for h in range(halves):
        out_ref[h * rows : (h + 1) * rows] = refs[h][0]


def assemble(outs):
    halves = len(outs)
    slots, rows, part, width = outs[0].shape
    return pl.pallas_call(
        functools.partial(assemble_kernel, halves),
        grid=(slots,),
        in_specs=[pl.BlockSpec((1, rows, part, width), lambda i: (i, 0, 0, 0))] * halves,
        out_specs=pl.BlockSpec((halves * rows, part, width), lambda i: (0, i, 0)),
        out_shape=jax.ShapeDtypeStruct((halves * rows, slots * part, width), bf16),
        compiler_params=pltpu.CompilerParams(vmem_limit_bytes=vmem_bytes),
    )(*outs)


def ocean_kernel(on_ref, start_ref, mask_ref, w_in, w_out, scale, head, next_ref, field_ref):
    half = w_in.shape[1] // 2
    fields = field_ref.shape[1]
    total = None
    for i in range(2):
        h = gelu(dot(on_ref[...], w_in[:, i * half : (i + 1) * half])).astype(bf16)
        part = dot(h, w_out[i * half : (i + 1) * half, :])
        total = part if total is None else total + part
    mask = mask_ref[...]
    out = (start_ref[...].astype(f32) + mask * (scale[...] * total)).astype(bf16)
    next_ref[...] = out
    parts = dot(out, head[...])
    field_ref[...] = mask * (
        parts[:, :fields] + parts[:, fields : 2 * fields] + parts[:, 2 * fields :]
    )


def ocean_mlp(on, start, mask, w_in, w_out, scale, head):
    cells, width = on.shape
    tile = pick(cells, 768)
    fields = head.shape[1]
    high = lax.reduce_precision(head, 8, 7)
    mid = lax.reduce_precision(head - high, 8, 7)
    heads = jnp.concatenate([high, mid, head - high - mid], axis=1).astype(bf16)
    rows = lambda n: pl.BlockSpec((tile, n), lambda i: (i, 0))
    return pl.pallas_call(
        ocean_kernel,
        grid=(cells // tile,),
        in_specs=[
            rows(width),
            rows(width),
            rows(1),
            whole(w_in.shape),
            whole(w_out.shape),
            whole((1, width)),
            whole(heads.shape),
        ],
        out_specs=[rows(width), rows(fields)],
        out_shape=[
            jax.ShapeDtypeStruct((cells, width), bf16),
            jax.ShapeDtypeStruct((cells, fields), f32),
        ],
        compiler_params=pltpu.CompilerParams(vmem_limit_bytes=vmem_bytes),
        cost_estimate=pl.CostEstimate(
            flops=4 * cells * width * w_in.shape[1],
            bytes_accessed=8 * cells * width,
            transcendentals=cells * w_in.shape[1],
        ),
    )(on, start, mask, w_in, w_out, scale[None], heads)


def phases(count_first, count_second, length):
    first_index = lax.broadcasted_iota(jnp.int32, (count_first, count_second), 0)
    second_index = lax.broadcasted_iota(jnp.int32, (count_first, count_second), 1)
    turns = first_index * second_index % length
    return turns.astype(f32) * (2.0 * math.pi / length)


def lon_matrices(longitudes, bands):
    kept = longitudes // 2
    scale = 1.0 / math.sqrt(longitudes)
    angles = phases(longitudes, kept, longitudes)
    cos, sin = jnp.cos(angles) * scale, jnp.sin(angles) * scale
    weight = jnp.where(lax.broadcasted_iota(jnp.int32, (1, kept), 1) == 0, 1.0, 2.0)
    shape = (longitudes, bands, kept // bands, 1)

    def laid(re, im):
        both = jnp.concatenate([re.reshape(shape), im.reshape(shape)], axis=-1)
        return both.reshape(longitudes, -1).astype(bf16)

    return laid(cos, -sin).T, laid(cos * weight, -sin * weight)


def lat_matrices(lats, bands, halves, pair):
    order = jnp.arange(lats).reshape(bands, halves, lats // (bands * halves * pair), pair)
    order = order.transpose(1, 3, 0, 2).reshape(halves * pair, -1)
    turns = jnp.arange(lats)[:, None] * order.reshape(1, lats) % lats
    angles = turns.astype(f32) * (2.0 * math.pi / lats)
    cos = jnp.cos(angles) / math.sqrt(lats)
    sin = jnp.sin(angles) / math.sqrt(lats)
    fwd = jnp.concatenate(
        [jnp.concatenate([cos, sin], axis=1), jnp.concatenate([-sin, cos], axis=1)], axis=0
    )
    cos_t = cos.T.reshape(halves * pair, -1, lats)
    sin_t = sin.T.reshape(halves * pair, -1, lats)
    back = jnp.concatenate(
        [
            jnp.concatenate([cos_t, -sin_t], axis=2),
            jnp.concatenate([sin_t, cos_t], axis=2),
        ],
        axis=1,
    ).reshape(2 * lats, 2 * lats)
    return fwd.astype(bf16), back.astype(bf16)


def dense_groups(weights):
    width, group = weights.shape[-2], weights.shape[-1]
    groups = width // group
    tiled = jnp.concatenate([weights] * groups, axis=-1)
    row = lax.broadcasted_iota(jnp.int32, (width, width), 0) // group
    column = lax.broadcasted_iota(jnp.int32, (width, width), 1) // group
    return jnp.where(row == column, tiled, 0.0).astype(bf16)


def to_band(x):
    return lax.all_to_all(x, "band", split_axis=0, concat_axis=0, tiled=True)


def to_quarter(x):
    return lax.all_to_all(x, quarter, split_axis=0, concat_axis=0, tiled=True)


def modes_of_bands(xs, fwd, back, weights, biases, pair, early):
    bands, count, parts, lanes = xs[0].shape
    xs = [to_band(x) for x in xs]
    xs = [x.transpose(2, 0, 1, 3).reshape(parts, bands * count, lanes) for x in xs]
    zs = mix_modes(xs, fwd, back, weights, biases, pair, early)
    zs = [z.reshape(parts // 2, 2, bands, count, lanes).transpose(2, 3, 0, 1, 4) for z in zs]
    return [z.reshape(bands, count, parts, lanes) for z in zs]


def with_halo(cells, sides, width, closed):
    for axis, dim in sides:
        count = lax.axis_size(axis)
        ends = count if closed else count - 1
        head = lax.slice_in_dim(cells, 0, width, axis=dim)
        tail = lax.slice_in_dim(cells, cells.shape[dim] - width, cells.shape[dim], axis=dim)
        cells = jnp.concatenate(
            [
                lax.ppermute(tail, axis, [(i, (i + 1) % count) for i in range(ends)]),
                cells,
                lax.ppermute(head, axis, [((i + 1) % count, i) for i in range(ends)]),
            ],
            axis=dim,
        )
    return cells


def on_device(
    atmosphere,
    spec_weight,
    spec_bias,
    norm_gain,
    norm_shift,
    fc_in,
    fc_out,
    flux_head,
    flux_embed,
    ocean_state,
    sea_mask,
    depth_kernel,
    ocean_gain,
    ocean_shift,
    ocean_in,
    ocean_out,
    layer_scale,
    field_head,
    patch_embed,
):
    column_index = lax.axis_index(quarter)
    slots = lax.axis_size(quarter)
    bands = lax.axis_size("band")
    rows, longitudes, slot = atmosphere.shape
    width_full = slot * slots
    part = longitudes // slots
    waves = longitudes // 2 // bands
    halves = 2 if rows % 4 == 0 else 1
    pair = 2 if rows % (2 * halves) == 0 else 1
    half = rows // halves
    lon_fwd, lon_back = lon_matrices(longitudes, bands)
    lat_fwd, lat_back = lat_matrices(rows * bands, bands, halves, pair)
    weights = dense_groups(spec_weight)
    biases = spec_bias[:, :, :, None, :]
    heads = lax.all_gather(flux_head, quarter, axis=0, tiled=True)
    embed = lax.all_gather(patch_embed, quarter, axis=1, tiled=True)
    gain = lambda b, i: norm_gain[b, i][None]
    shift = lambda b, i: norm_shift[b, i][None]
    cut = lambda x, h: lax.slice_in_dim(x, h * half, (h + 1) * half)
    in0, out0 = gathered_pairs(fc_in[0], fc_out[0], ("comp", "tile"))
    in1, out1 = gathered_pairs(fc_in[1], fc_out[1], ("comp", "tile"))

    values = atmosphere.astype(f32)
    sums = jnp.stack([jnp.sum(values, axis=-1), jnp.sum(values * values, axis=-1)])
    sums = shift_sum(sums, ("tile", "comp")) / width_full
    rstd = lax.rsqrt(sums[1] - sums[0] * sums[0] + eps_norm)
    stats = jnp.stack([sums[0], rstd] + [jnp.zeros_like(rstd)] * 6, axis=1)
    scaling = lax.dynamic_slice_in_dim(norm_gain[0, 0], column_index * slot, slot)[None]
    offset = lax.dynamic_slice_in_dim(norm_shift[0, 0], column_index * slot, slot)[None]
    streams = [cut(atmosphere, h) for h in range(halves)]
    stats = [(cut(stats, h), scaling, offset) for h in range(halves)]
    spectra = [
        lon_forward(streams[h], lon_fwd, bands, waves, pair, stats[h]) for h in range(halves)
    ]
    spectra = modes_of_bands(
        spectra, lat_fwd, lat_back, weights[0], biases[0], pair, in0 + out0
    )
    spectra = [to_band(z) for z in spectra]
    after_one, fluxes = [], []
    for h in range(halves):
        u = lon_back_call(
            spectra[h], lon_back, slots, pair, streams[h], stats[h], in1 + out1 if h == 0 else ()
        )
        u = to_quarter(u).reshape(slots, half * part, slot)
        a, f = first_mlp(u, gain(0, 1), shift(0, 1), heads, in0, out0)
        after_one.append(a)
        fluxes.append(f.reshape(half, part, -1))

    fluxes = jnp.concatenate(fluxes, axis=0)
    upsampled = jnp.repeat(jnp.repeat(fluxes, 2, axis=0), 2, axis=1)
    sea_cells = sea_mask.astype(f32)[..., None]
    forcing = jnp.einsum("ijf,fc->ijc", upsampled, flux_embed, precision=full_precision)
    start = (ocean_state.astype(f32) + sea_cells * forcing).astype(bf16)
    widened = with_halo(start, ((quarter, 1),), 3, True)
    extended = with_halo(widened, (("band", 0),), 3, False)
    tile_rows = start.shape[0] // halves
    tile_columns = start.shape[1]
    cells = tile_rows * tile_columns
    nexts, surfaces, middles, spectra = [], [], [], []
    for h in range(halves):
        first = h * tile_rows
        convolved = jnp.zeros((tile_rows,) + start.shape[1:], f32)
        for row_step in range(7):
            for col_step in range(7):
                convolved = (
                    convolved
                    + extended[
                        first + row_step : first + row_step + tile_rows,
                        col_step : col_step + tile_columns,
                    ].astype(f32)
                    * depth_kernel[row_step, col_step]
                )
        normed = layer_norm(convolved, ocean_gain, ocean_shift).astype(bf16)
        ocean_next, surface = ocean_mlp(
            normed.reshape(cells, -1),
            start[first : first + tile_rows].reshape(cells, -1),
            sea_cells[first : first + tile_rows].reshape(cells, 1),
            ocean_in,
            ocean_out,
            layer_scale,
            field_head,
        )
        nexts.append(ocean_next.reshape((tile_rows,) + start.shape[1:]))
        surface = surface.reshape(tile_rows, tile_columns, -1)
        surfaces.append(surface)
        patches = (
            surface.reshape(half, 2, part, 2, surface.shape[2])
            .transpose(0, 2, 4, 1, 3)
            .reshape(half * part, -1)
        )
        middle, normed = make_middle(
            after_one[h],
            product_left(patches),
            product_right(embed),
            gain(1, 0),
            shift(1, 0),
            slots,
        )
        middles.append(middle)
        normed = to_quarter(normed).reshape(slots, half, part, slot)
        spectra.append(lon_forward(normed, lon_fwd, bands, waves, pair))
    ocean_next = jnp.concatenate(nexts, axis=0)
    surface = jnp.concatenate(surfaces, axis=0)

    spectra = modes_of_bands(spectra, lat_fwd, lat_back, weights[1], biases[1], pair, [])
    spectra = [to_band(z) for z in spectra]
    outs = []
    for h in range(halves):
        restored = lon_back_call(spectra[h], lon_back, slots, pair)
        restored = to_quarter(restored).reshape(slots, half * part, slot)
        out = second_mlp(
            middles[h], restored, gain(1, 0), shift(1, 0), gain(1, 1), shift(1, 1), in1, out1
        )
        outs.append(to_quarter(out).reshape(slots, half, part, slot))
    return (assemble(outs), ocean_next, surface)


def solution(mesh):
    placed = (
        P("band", None, ("comp", "tile")),
        P(None, None, None, ("comp", "tile"), None),
        P(None, None, None, ("comp", "tile")),
        P(),
        P(),
        P(None, None, ("comp", "tile")),
        P(None, ("comp", "tile"), None),
        P(("comp", "tile"), None),
        P(),
        P("band", ("comp", "tile"), None),
        P("band", ("comp", "tile")),
        P(),
        P(),
        P(),
        P(),
        P(),
        P(),
        P(),
        P(None, ("comp", "tile")),
    )
    return jax.shard_map(
        on_device,
        mesh=mesh,
        in_specs=placed,
        out_specs=(
            P("band", None, ("comp", "tile")),
            P("band", ("comp", "tile"), None),
            P("band", ("comp", "tile"), None),
        ),
        check_vma=False,
    )
```

```python
import functools
import math

import jax
import jax.numpy as jnp
import numpy as np
from jax import lax
from jax.experimental import pallas as pl
from jax.experimental.pallas import tpu as pltpu
from jax.sharding import PartitionSpec as P

full_precision = lax.Precision.HIGHEST
eps_norm = 1e-06
shrink_level = 0.01
f32 = jnp.float32
bf16 = jnp.bfloat16
quarter = ("comp", "tile")
vmem_bytes = 56 * 1024 * 1024

tail_log2 = (
    -0.9999930608094244,
    -1.1512017040487785,
    -0.45877096697476855,
    -0.053412112881497276,
    0.008080722210665518,
    -0.0007692214388919801,
    3.309301407796759e-05,
)
tail_end = 6.0


def gelu(x):
    a = jnp.minimum(jnp.abs(x), tail_end)
    power = tail_log2[-1] * a + tail_log2[-2]
    for c in tail_log2[-3::-1]:
        power = power * a + c
    return jnp.maximum(x, 0.0) - a * jnp.exp2(power)


def pick(n, cap):
    for t in range(cap, 0, -16):
        if n % t == 0:
            return t
    return n


def pick_rows(tokens, part):
    rows = tokens // part
    return part * max(n for n in range(1, rows + 1) if rows % n == 0 and n * part <= 384)


def dot(a, b):
    return jnp.dot(a, b, preferred_element_type=f32)


def layer_norm(values, scaling, offset):
    average = jnp.mean(values, axis=-1, keepdims=True)
    squares = jnp.mean(values * values, axis=-1, keepdims=True)
    variance = squares - average * average
    return (values - average) * lax.rsqrt(variance + eps_norm) * scaling + offset


def split3(x, axis):
    high = lax.reduce_precision(x, 8, 7)
    low = x - high
    return high.astype(bf16), lax.reduce_precision(low, 8, 7).astype(bf16)


def product_left(x):
    high, low = split3(x, -1)
    return jnp.concatenate([high, low, high], axis=-1)


def product_right(x):
    high, low = split3(x, 0)
    return jnp.concatenate([high, high, low], axis=0)


def whole(shape):
    return pl.BlockSpec(shape, lambda *_: (0,) * len(shape))


def shift_sum(x, axes):
    for axis in axes:
        n = lax.axis_size(axis)
        mine = x
        for d in range(1, n):
            x = x + lax.ppermute(mine, axis, [(i, (i + d) % n) for i in range(n)])
    return x


def spread(x, index, count):
    mine = lax.broadcasted_iota(jnp.int32, (count,) + (1,) * x.ndim, 0) == index
    return shift_sum(jnp.where(mine, x[None], jnp.zeros((), x.dtype)), ("tile", "comp"))


def gathered(x, axes):
    parts = [x]
    for axis in axes:
        n = lax.axis_size(axis)
        parts = parts + [
            lax.ppermute(part, axis, [(i, (i + d) % n) for i in range(n)])
            for d in range(1, n)
            for part in parts
        ]
    return parts


def gathered_pairs(x, y, axes):
    return gathered(x, axes), gathered(y, axes)


def mlp_rows(filtered, gain, shift, w_in, w_out):
    n2 = layer_norm(filtered, gain, shift).astype(bf16)
    total = filtered
    for a, b in zip(w_in, w_out):
        total = total + dot(gelu(dot(n2, a[...])).astype(bf16), b[...])
    return total.astype(bf16)


def first_mlp_kernel(n, u_ref, gain, shift, head, *refs):
    w_in, w_out, (out_ref, flux_ref) = refs[:n], refs[n : 2 * n], refs[2 * n :]
    u = jnp.concatenate([u_ref[i].astype(f32) for i in range(u_ref.shape[0])], axis=-1)
    out = mlp_rows(u, gain[...], shift[...], w_in, w_out)
    out_ref[...] = out
    flux_ref[...] = dot(out, head[...])


def first_mlp(u, gain, shift, head, w_in, w_out):
    slots, tokens, width = u.shape
    full = slots * width
    tile = pick(tokens, 384)
    n = len(w_in)
    hidden = sum(w.shape[1] for w in w_in)
    return pl.pallas_call(
        functools.partial(first_mlp_kernel, n),
        grid=(tokens // tile,),
        in_specs=[
            pl.BlockSpec((slots, tile, width), lambda i: (0, i, 0)),
            whole((1, full)),
            whole((1, full)),
            whole(head.shape),
        ]
        + [whole(w.shape) for w in w_in]
        + [whole(w.shape) for w in w_out],
        out_specs=[
            pl.BlockSpec((tile, full), lambda i: (i, 0)),
            pl.BlockSpec((tile, head.shape[1]), lambda i: (i, 0)),
        ],
        out_shape=[
            jax.ShapeDtypeStruct((tokens, full), bf16),
            jax.ShapeDtypeStruct((tokens, head.shape[1]), f32),
        ],
        compiler_params=pltpu.CompilerParams(vmem_limit_bytes=vmem_bytes),
        cost_estimate=pl.CostEstimate(
            flops=4 * tokens * full * hidden,
            bytes_accessed=4 * tokens * full + 4 * full * hidden,
            transcendentals=tokens * hidden,
        ),
    )(u, gain, shift, head, *w_in, *w_out)


def second_mlp_kernel(n, v_ref, r_ref, gain0, shift0, gain, shift, *refs):
    w_in, w_out, out_ref = refs[:n], refs[n : 2 * n], refs[2 * n]
    v = v_ref[...].astype(f32)
    r = jnp.concatenate([r_ref[i].astype(f32) for i in range(r_ref.shape[0])], axis=-1)
    u = (v + r + layer_norm(v, gain0[...], shift0[...])).astype(bf16).astype(f32)
    out = mlp_rows(u, gain[...], shift[...], w_in, w_out)
    width = out_ref.shape[3]
    for i in range(out_ref.shape[0]):
        out_ref[i] = out[:, i * width : (i + 1) * width].reshape(out_ref.shape[1:])


def second_mlp(v, r, gain0, shift0, gain, shift, w_in, w_out, part):
    slots, tokens, width = r.shape
    full = slots * width
    tile = pick_rows(tokens, part)
    n = len(w_in)
    hidden = sum(w.shape[1] for w in w_in)
    return pl.pallas_call(
        functools.partial(second_mlp_kernel, n),
        grid=(tokens // tile,),
        in_specs=[
            pl.BlockSpec((tile, full), lambda i: (i, 0)),
            pl.BlockSpec((slots, tile, width), lambda i: (0, i, 0)),
        ]
        + [whole((1, full))] * 4
        + [whole(w.shape) for w in w_in]
        + [whole(w.shape) for w in w_out],
        out_specs=pl.BlockSpec((slots, tile // part, part, width), lambda i: (0, i, 0, 0)),
        out_shape=jax.ShapeDtypeStruct((slots, tokens // part, part, width), bf16),
        compiler_params=pltpu.CompilerParams(vmem_limit_bytes=vmem_bytes),
        cost_estimate=pl.CostEstimate(
            flops=4 * tokens * full * hidden,
            bytes_accessed=6 * tokens * full + 4 * full * hidden,
            transcendentals=tokens * hidden,
        ),
    )(v, r, gain0, shift0, gain, shift, *w_in, *w_out)


def middle_kernel(a_ref, p_ref, e_ref, gain, shift, v_ref, n_ref):
    v = (a_ref[...].astype(f32) + dot(p_ref[...], e_ref[...])).astype(bf16)
    v_ref[...] = v
    normed = layer_norm(v.astype(f32), gain[...], shift[...]).astype(bf16)
    width = n_ref.shape[3]
    for i in range(n_ref.shape[0]):
        n_ref[i] = normed[:, i * width : (i + 1) * width].reshape(n_ref.shape[1:])


def make_middle(a, patches, embed, gain, shift, slots, part):
    tokens, full = a.shape
    tile = pick_rows(tokens, part)
    return pl.pallas_call(
        middle_kernel,
        grid=(tokens // tile,),
        in_specs=[
            pl.BlockSpec((tile, full), lambda i: (i, 0)),
            pl.BlockSpec((tile, patches.shape[1]), lambda i: (i, 0)),
            whole(embed.shape),
            whole((1, full)),
            whole((1, full)),
        ],
        out_specs=[
            pl.BlockSpec((tile, full), lambda i: (i, 0)),
            pl.BlockSpec((slots, tile // part, part, full // slots), lambda i: (0, i, 0, 0)),
        ],
        out_shape=[
            jax.ShapeDtypeStruct((tokens, full), bf16),
            jax.ShapeDtypeStruct((slots, tokens // part, part, full // slots), bf16),
        ],
        compiler_params=pltpu.CompilerParams(vmem_limit_bytes=vmem_bytes),
    )(a, patches, embed, gain, shift)


def soft_shrink(y):
    return y - jnp.clip(y, -shrink_level, shrink_level)


def modes_kernel(halves, pair, x_refs, fwd, back, weights, biases, z_refs):
    width = weights.shape[2]
    waves = z_refs[0].shape[0]
    for k in range(waves):
        x = jnp.concatenate(
            [
                x_refs[h][2 * k + part, :, j * width : (j + 1) * width]
                for part in range(2)
                for h in range(halves)
                for j in range(pair)
            ],
            axis=0,
        )
        lats = x.shape[0] // 2
        s = dot(fwd[...], x).astype(bf16)
        for layer in range(2):
            s_re, s_im = s[:lats], s[lats:]
            y_re = dot(s_re, weights[layer, 0]) - dot(s_im, weights[layer, 1])
            y_im = dot(s_im, weights[layer, 0]) + dot(s_re, weights[layer, 1])
            y_re = y_re + biases[layer, 0]
            y_im = y_im + biases[layer, 1]
            if layer == 0:
                y_re, y_im = jnp.maximum(y_re, 0.0), jnp.maximum(y_im, 0.0)
            else:
                y_re, y_im = soft_shrink(y_re), soft_shrink(y_im)
            s = jnp.concatenate([y_re.astype(bf16), y_im.astype(bf16)], axis=0)
        z = dot(back[...], s)
        rows = z.shape[0] // (halves * pair)
        for h in range(halves):
            cut = [z[(h * pair + j) * rows : (h * pair + j + 1) * rows] for j in range(pair)]
            z_refs[h][k] = jnp.concatenate(cut, axis=-1).astype(bf16)


def mix_modes(xs, fwd, back, weights, biases, pair, early):
    halves = len(xs)
    parts, rows, lanes = xs[0].shape
    waves = parts // 2
    lats = fwd.shape[0] // 2
    width = lanes // pair
    step = 3 if waves % 3 == 0 else 1

    def kernel(*refs):
        x_refs, refs = refs[:halves], refs[halves:]
        z_refs = refs[4 + len(early) :]
        modes_kernel(halves, pair, x_refs, *refs[:4], z_refs)

    return pl.pallas_call(
        kernel,
        grid=(waves // step,),
        in_specs=[pl.BlockSpec((2 * step, rows, lanes), lambda i: (i, 0, 0))] * halves
        + [whole(fwd.shape), whole(back.shape), whole(weights.shape), whole(biases.shape)]
        + [pl.BlockSpec(memory_space=pl.ANY)] * len(early),
        out_specs=[pl.BlockSpec((step, 2 * rows, lanes), lambda i: (i, 0, 0))] * halves,
        out_shape=[jax.ShapeDtypeStruct((waves, 2 * rows, lanes), bf16)] * halves,
        compiler_params=pltpu.CompilerParams(vmem_limit_bytes=vmem_bytes),
        cost_estimate=pl.CostEstimate(
            flops=waves * 16 * (lats * lats * width + lats * width * width),
            bytes_accessed=8 * waves * lats * width,
            transcendentals=0,
        ),
    )(*xs, fwd, back, weights, biases, *early)


def norm_with(values, stats, scaling, offset):
    column = jnp.transpose(stats)
    return (values - column[:, 0:1]) * column[:, 1:2] * scaling + offset


def aligned(waves):
    return 2 * waves % 16 == 0


def spectrum_block(bands, waves, lanes):
    if aligned(waves):
        return pl.BlockSpec((bands, 1, 2 * waves, lanes), lambda i: (0, i, 0, 0))
    return pl.BlockSpec((1, bands * 2 * waves, lanes), lambda i: (i, 0, 0))


def lon_forward(source, matrix, bands, waves, pair, stats=None):
    if stats is None:
        _, rows, part, width = source.shape
    else:
        rows, longitudes, width = source.shape
    lanes = pair * width

    def kernel(*refs):
        x_ref, f_ref, out_ref = refs[0], refs[1], refs[-1]
        columns = []
        for j in range(pair):
            if stats is None:
                columns.append(
                    jnp.concatenate([x_ref[i, j] for i in range(x_ref.shape[0])], axis=0)
                )
            else:
                st_ref, gain, shift = refs[2:5]
                normed = norm_with(x_ref[j].astype(f32), st_ref[j], gain[...], shift[...])
                columns.append(normed.astype(bf16))
        y = dot(f_ref[...], jnp.concatenate(columns, axis=-1)).astype(bf16)
        if aligned(waves):
            out_ref[:, 0] = y.reshape(bands, 2 * waves, lanes)
        else:
            out_ref[0] = y

    if stats is None:
        args = (source, matrix)
        specs = [
            pl.BlockSpec((source.shape[0], pair, part, width), lambda i: (0, i, 0, 0)),
            whole(matrix.shape),
        ]
    else:
        st, gain, shift = stats
        args = (source, matrix, st, gain, shift)
        specs = [
            pl.BlockSpec((pair, longitudes, width), lambda i: (i, 0, 0)),
            whole(matrix.shape),
            pl.BlockSpec((pair, st.shape[1], longitudes), lambda i: (i, 0, 0)),
            whole(gain.shape),
            whole(shift.shape),
        ]
    count = rows // pair
    if aligned(waves):
        shape = (bands, count, 2 * waves, lanes)
    else:
        shape = (count, bands * 2 * waves, lanes)
    out = pl.pallas_call(
        kernel,
        grid=(count,),
        in_specs=specs,
        out_specs=spectrum_block(bands, waves, lanes),
        out_shape=jax.ShapeDtypeStruct(shape, bf16),
        compiler_params=pltpu.CompilerParams(vmem_limit_bytes=vmem_bytes),
        cost_estimate=pl.CostEstimate(
            flops=2 * rows * matrix.shape[0] * matrix.shape[1] * width,
            bytes_accessed=4 * rows * matrix.shape[0] * width,
            transcendentals=0,
        ),
    )(*args)
    if not aligned(waves):
        out = out.reshape(count, bands, 2 * waves, lanes).transpose(1, 0, 2, 3)
    return out


def lon_back_call(z, matrix, slots, pair, source=None, stats=None, early=()):
    bands, count, parts, lanes = z.shape
    waves = parts // 2
    width = lanes // pair
    longitudes = matrix.shape[0]
    part = longitudes // slots
    if not aligned(waves):
        z = z.transpose(1, 0, 2, 3).reshape(count, bands * parts, lanes)

    def kernel(*refs):
        z_ref, g_ref, out_ref = refs[0], refs[1], refs[-1]
        spectra = z_ref[:, 0].reshape(bands * parts, lanes) if aligned(waves) else z_ref[0]
        r = dot(g_ref[...], spectra)
        for j in range(pair):
            u = r[:, j * width : (j + 1) * width]
            if stats is not None:
                v_ref, st_ref, gain, shift = refs[2:6]
                v = v_ref[j].astype(f32)
                u = v + u + norm_with(v, st_ref[j], gain[...], shift[...])
            u = u.astype(bf16)
            for i in range(slots):
                out_ref[i, j] = u[i * part : (i + 1) * part]

    args = [z, matrix]
    specs = [spectrum_block(bands, waves, lanes), whole(matrix.shape)]
    if stats is not None:
        st, gain, shift = stats
        args += [source, st, gain, shift]
        specs += [
            pl.BlockSpec((pair, longitudes, width), lambda i: (i, 0, 0)),
            pl.BlockSpec((pair, st.shape[1], longitudes), lambda i: (i, 0, 0)),
            whole(gain.shape),
            whole(shift.shape),
        ]
    return pl.pallas_call(
        kernel,
        grid=(count,),
        in_specs=specs + [pl.BlockSpec(memory_space=pl.ANY)] * len(early),
        out_specs=pl.BlockSpec((slots, pair, part, width), lambda i: (0, i, 0, 0)),
        out_shape=jax.ShapeDtypeStruct((slots, count * pair, part, width), bf16),
        compiler_params=pltpu.CompilerParams(vmem_limit_bytes=vmem_bytes),
        cost_estimate=pl.CostEstimate(
            flops=2 * count * longitudes * bands * parts * lanes,
            bytes_accessed=6 * count * longitudes * lanes,
            transcendentals=0,
        ),
    )(*args, *early)


def assemble_kernel(halves, *refs):
    out_ref = refs[halves]
    rows = refs[0].shape[1]
    for h in range(halves):
        out_ref[h * rows : (h + 1) * rows] = refs[h][0]


def assemble(outs):
    halves = len(outs)
    slots, rows, part, width = outs[0].shape
    return pl.pallas_call(
        functools.partial(assemble_kernel, halves),
        grid=(slots,),
        in_specs=[pl.BlockSpec((1, rows, part, width), lambda i: (i, 0, 0, 0))] * halves,
        out_specs=pl.BlockSpec((halves * rows, part, width), lambda i: (0, i, 0)),
        out_shape=jax.ShapeDtypeStruct((halves * rows, slots * part, width), bf16),
        compiler_params=pltpu.CompilerParams(vmem_limit_bytes=vmem_bytes),
    )(*outs)


def ocean_block(extended, taps, gain, shift, mask, w_in, w_out, scale, head, early):
    lane = 128
    size = taps.shape[0]
    reach = size // 2
    side = -(-reach // 8) * 8
    columns = extended.shape[1] - 2 * side
    rows = extended.shape[0] - 2 * reach
    width = extended.shape[2]
    lane_parts = width // lane
    blocks = 16 // lane_parts
    block = columns // blocks
    span = block + 2 * side
    tile = blocks * lane_parts
    fields = head.shape[1]
    step = max(n for n in range(1, 5) if rows % n == 0)
    group = 4

    taps = taps.reshape(size * size, 1, lane_parts, lane)
    taps = jnp.broadcast_to(taps, (size * size, blocks, lane_parts, lane))
    taps = taps.reshape(size * size, tile, lane).astype(bf16)
    high = lax.reduce_precision(head, 8, 7)
    mid = lax.reduce_precision(head - high, 8, 7)
    heads = jnp.concatenate([high, mid, head - high - mid], axis=1).astype(bf16)

    def kernel(*refs):
        x_ref, t_ref, gain, shift, mask_ref, w_in, w_out, scale, head = refs[:9]
        next_ref, field_ref, laid, held, summed, normed = refs[9 + len(early) :]
        at = pl.program_id(0)

        @pl.when(at == 0)
        def _():
            def lay(r, carry):
                row = x_ref[r].astype(f32)
                for b in range(blocks):
                    for p in range(lane_parts):
                        held[pl.ds(b * lane_parts + p, span, stride=tile), :] = row[
                            b * block : b * block + span, p * lane : (p + 1) * lane
                        ]
                laid[r] = held[...].astype(bf16)
                return carry

            lax.fori_loop(0, rows + 2 * reach, lay, 0)

        def correlate(r, carry):
            for first in range(0, block, group):
                count = min(group, block - first)
                total = [None] * count
                for a in range(size):
                    near = [
                        laid[at * step + r + a, pl.ds((side - reach + first + t) * tile, tile), :]
                        for t in range(count + size - 1)
                    ]
                    for q in range(count):
                        part = near[q] * t_ref[a * size]
                        for e in range(1, size):
                            part = part + near[q + e] * t_ref[a * size + e]
                        part = part.astype(f32)
                        total[q] = part if total[q] is None else total[q] + part
                for q in range(count):
                    summed[pl.ds((first + q) * tile, tile), :] = total[q]
            for b in range(blocks):
                cut = [
                    summed[pl.ds(b * lane_parts + p, block, stride=tile), :]
                    for p in range(lane_parts)
                ]
                cells = jnp.concatenate(cut, axis=-1)
                normed[r, b * block : (b + 1) * block] = layer_norm(cells, gain[...], shift[...])
            return carry

        lax.fori_loop(0, step, correlate, 0)
        cells = normed[...].reshape(step * columns, width).astype(bf16)
        half = w_in.shape[1] // 2
        update = None
        for i in range(2):
            h = gelu(dot(cells, w_in[:, i * half : (i + 1) * half])).astype(bf16)
            part = dot(h, w_out[i * half : (i + 1) * half, :])
            update = part if update is None else update + part
        mask = mask_ref[...]
        first = at * step + reach
        start = x_ref[pl.ds(first, step), side : side + columns, :].astype(f32)
        start = start.reshape(step * columns, width)
        out = (start + mask * (scale[...] * update)).astype(bf16)
        next_ref[...] = out
        parts = dot(out, head[...])
        field_ref[...] = mask * (
            parts[:, :fields] + parts[:, fields : 2 * fields] + parts[:, 2 * fields :]
        )

    cells = rows * columns
    by_cell = lambda n: pl.BlockSpec((step * columns, n), lambda i: (i, 0))
    return pl.pallas_call(
        kernel,
        grid=(rows // step,),
        in_specs=[
            whole(extended.shape),
            whole(taps.shape),
            whole((1, width)),
            whole((1, width)),
            by_cell(1),
            whole(w_in.shape),
            whole(w_out.shape),
            whole((1, width)),
            whole(heads.shape),
        ]
        + [pl.BlockSpec(memory_space=pl.ANY)] * len(early),
        out_specs=[by_cell(width), by_cell(fields)],
        out_shape=[
            jax.ShapeDtypeStruct((cells, width), bf16),
            jax.ShapeDtypeStruct((cells, fields), f32),
        ],
        scratch_shapes=[
            pltpu.VMEM((rows + 2 * reach, span * tile, lane), bf16),
            pltpu.VMEM((span * tile, lane), f32),
            pltpu.VMEM((block * tile, lane), f32),
            pltpu.VMEM((step, columns, width), f32),
        ],
        compiler_params=pltpu.CompilerParams(vmem_limit_bytes=vmem_bytes),
        cost_estimate=pl.CostEstimate(
            flops=4 * cells * width * w_in.shape[1] + 100 * cells * width,
            bytes_accessed=8 * cells * width,
            transcendentals=cells * w_in.shape[1],
        ),
    )(extended, taps, gain[None], shift[None], mask, w_in, w_out, scale[None], heads, *early)


def lon_matrices(longitudes, bands):
    kept = longitudes // 2
    scale = 1.0 / math.sqrt(longitudes)
    turns = np.arange(longitudes)[:, None] * np.arange(kept)[None] % longitudes
    angles = turns * (2.0 * math.pi / longitudes)
    cos, sin = np.cos(angles) * scale, np.sin(angles) * scale
    weight = np.where(np.arange(kept) == 0, 1.0, 2.0)[None]

    def laid(re, im):
        return np.stack([re, im], axis=-1).reshape(longitudes, -1)

    fwd = np.ascontiguousarray(laid(cos, -sin).T)
    back = laid(cos * weight, -sin * weight)
    return jnp.asarray(fwd, bf16), jnp.asarray(back, bf16)


def lat_matrices(lats, bands, halves, pair):
    order = np.arange(lats).reshape(bands, halves, lats // (bands * halves * pair), pair)
    order = order.transpose(1, 3, 0, 2).reshape(1, lats)
    angles = (np.arange(lats)[:, None] * order % lats) * (2.0 * math.pi / lats)
    cos = np.cos(angles) / math.sqrt(lats)
    sin = np.sin(angles) / math.sqrt(lats)
    fwd = np.block([[cos, sin], [-sin, cos]])
    cos_t = cos.T.reshape(halves * pair, -1, lats)
    sin_t = sin.T.reshape(halves * pair, -1, lats)
    back = np.concatenate(
        [np.concatenate([cos_t, -sin_t], axis=2), np.concatenate([sin_t, cos_t], axis=2)], axis=1
    ).reshape(2 * lats, 2 * lats)
    return jnp.asarray(fwd, bf16), jnp.asarray(back, bf16)


def dense_groups(weights):
    width, group = weights.shape[-2], weights.shape[-1]
    groups = width // group
    tiled = jnp.concatenate([weights] * groups, axis=-1)
    row = lax.broadcasted_iota(jnp.int32, (width, width), 0) // group
    column = lax.broadcasted_iota(jnp.int32, (width, width), 1) // group
    return jnp.where(row == column, tiled, 0.0).astype(bf16)


def to_band(x):
    return lax.all_to_all(x, "band", split_axis=0, concat_axis=0, tiled=True)


def to_quarter(x):
    return lax.all_to_all(x, quarter, split_axis=0, concat_axis=0, tiled=True)


def modes_of_bands(xs, fwd, back, weights, biases, pair, early):
    bands, count, parts, lanes = xs[0].shape
    xs = [to_band(x) for x in xs]
    xs = [x.transpose(2, 0, 1, 3).reshape(parts, bands * count, lanes) for x in xs]
    zs = mix_modes(xs, fwd, back, weights, biases, pair, early)
    zs = [z.reshape(parts // 2, 2, bands, count, lanes).transpose(2, 3, 0, 1, 4) for z in zs]
    return [z.reshape(bands, count, parts, lanes) for z in zs]


def with_halo(cells, reach):
    side = -(-reach // 8) * 8
    count = lax.axis_size(quarter)
    right = [(i, (i + 1) % count) for i in range(count)]
    left = [((i + 1) % count, i) for i in range(count)]
    before = lax.ppermute(cells[:, -reach:], quarter, right)
    after = lax.ppermute(cells[:, :reach], quarter, left)
    blank = jnp.zeros((cells.shape[0], side - reach, cells.shape[2]), cells.dtype)
    wide = lambda r: jnp.concatenate([blank[r], before[r], cells[r], after[r], blank[r]], axis=1)
    count = lax.axis_size("band")
    down = [(i, i + 1) for i in range(count - 1)]
    up = [(i + 1, i) for i in range(count - 1)]
    above = lax.ppermute(wide(slice(-reach, None)), "band", down)
    below = lax.ppermute(wide(slice(0, reach)), "band", up)
    return jnp.concatenate([above, wide(slice(None)), below], axis=0)


def on_device(
    atmosphere,
    spec_weight,
    spec_bias,
    norm_gain,
    norm_shift,
    fc_in,
    fc_out,
    flux_head,
    flux_embed,
    ocean_state,
    sea_mask,
    depth_kernel,
    ocean_gain,
    ocean_shift,
    ocean_in,
    ocean_out,
    layer_scale,
    field_head,
    patch_embed,
):
    column_index = lax.axis_index(quarter)
    slots = lax.axis_size(quarter)
    bands = lax.axis_size("band")
    rows, longitudes, slot = atmosphere.shape
    width_full = slot * slots
    part = longitudes // slots
    waves = longitudes // 2 // bands
    halves = 2 if rows % 4 == 0 else 1
    pair = 2 if rows % (2 * halves) == 0 else 1
    half = rows // halves
    lon_fwd, lon_back = lon_matrices(longitudes, bands)
    lat_fwd, lat_back = lat_matrices(rows * bands, bands, halves, pair)
    weights = dense_groups(spec_weight)
    biases = spec_bias[:, :, :, None, :]
    heads = spread(flux_head, column_index, slots).reshape(-1, flux_head.shape[1])
    embed = spread(patch_embed, column_index, slots).transpose(1, 0, 2)
    embed = product_right(embed.reshape(patch_embed.shape[0], -1))
    gain = lambda b, i: norm_gain[b, i][None]
    shift = lambda b, i: norm_shift[b, i][None]
    cut = lambda x, h: lax.slice_in_dim(x, h * half, (h + 1) * half)
    in0, out0 = gathered_pairs(fc_in[0], fc_out[0], ("comp", "tile"))
    in1, out1 = gathered_pairs(fc_in[1], fc_out[1], ("comp", "tile"))

    values = atmosphere.astype(f32)
    sums = jnp.stack([jnp.sum(values, axis=-1), jnp.sum(values * values, axis=-1)])
    sums = shift_sum(sums, ("tile", "comp")) / width_full
    rstd = lax.rsqrt(sums[1] - sums[0] * sums[0] + eps_norm)
    stats = jnp.stack([sums[0], rstd] + [jnp.zeros_like(rstd)] * 6, axis=1)
    scaling = lax.dynamic_slice_in_dim(norm_gain[0, 0], column_index * slot, slot)[None]
    offset = lax.dynamic_slice_in_dim(norm_shift[0, 0], column_index * slot, slot)[None]
    streams = [cut(atmosphere, h) for h in range(halves)]
    stats = [(cut(stats, h), scaling, offset) for h in range(halves)]
    spectra = [
        lon_forward(streams[h], lon_fwd, bands, waves, pair, stats[h]) for h in range(halves)
    ]
    spectra = modes_of_bands(
        spectra, lat_fwd, lat_back, weights[0], biases[0], pair, in0 + out0 + [heads, embed]
    )
    spectra = [to_band(z) for z in spectra]
    after_one, fluxes = [], []
    for h in range(halves):
        u = lon_back_call(
            spectra[h], lon_back, slots, pair, streams[h], stats[h], in1 + out1 if h == 0 else ()
        )
        u = to_quarter(u).reshape(slots, half * part, slot)
        a, f = first_mlp(u, gain(0, 1), shift(0, 1), heads, in0, out0)
        after_one.append(a)
        fluxes.append(f.reshape(half, part, -1))

    fluxes = jnp.concatenate(fluxes, axis=0)
    upsampled = jnp.repeat(jnp.repeat(fluxes, 2, axis=0), 2, axis=1)
    sea_cells = sea_mask.astype(f32)[..., None]
    forcing = jnp.einsum("ijf,fc->ijc", upsampled, flux_embed, precision=full_precision)
    start = (ocean_state.astype(f32) + sea_cells * forcing).astype(bf16)
    reach = depth_kernel.shape[0] // 2
    extended = with_halo(start, reach)
    tile_columns = start.shape[1]
    pieces = 2 if halves == 2 and half % 2 == 0 else 1
    tile_rows = start.shape[0] // (halves * pieces)
    cells = tile_rows * tile_columns
    nexts, surfaces, middles, spectra = [], [], [], []
    for h in range(halves):
        patches = []
        for piece in range(pieces):
            first = (h * pieces + piece) * tile_rows
            ocean_next, surface = ocean_block(
                extended[first : first + tile_rows + 2 * reach],
                depth_kernel,
                ocean_gain,
                ocean_shift,
                sea_cells[first : first + tile_rows].reshape(cells, 1),
                ocean_in,
                ocean_out,
                layer_scale,
                field_head,
                spectra[:1] if piece == pieces - 1 else [],
            )
            nexts.append(ocean_next.reshape((tile_rows,) + start.shape[1:]))
            surface = surface.reshape(tile_rows, tile_columns, -1)
            surfaces.append(surface)
            patches.append(
                surface.reshape(tile_rows // 2, 2, part, 2, surface.shape[2])
                .transpose(0, 2, 4, 1, 3)
                .reshape(tile_rows // 2 * part, -1)
            )
        middle, normed = make_middle(
            after_one[h],
            product_left(jnp.concatenate(patches, axis=0)),
            embed,
            gain(1, 0),
            shift(1, 0),
            slots,
            part,
        )
        middles.append(middle)
        spectra.append(lon_forward(to_quarter(normed), lon_fwd, bands, waves, pair))
    ocean_next = jnp.concatenate(nexts, axis=0)
    surface = jnp.concatenate(surfaces, axis=0)

    spectra = modes_of_bands(spectra, lat_fwd, lat_back, weights[1], biases[1], pair, [])
    spectra = [to_band(z) for z in spectra]
    outs = []
    for h in range(halves):
        restored = lon_back_call(spectra[h], lon_back, slots, pair)
        restored = to_quarter(restored).reshape(slots, half * part, slot)
        out = second_mlp(
            middles[h], restored, gain(1, 0), shift(1, 0), gain(1, 1), shift(1, 1), in1, out1, part
        )
        outs.append(to_quarter(out))
    return (assemble(outs), ocean_next, surface)


def solution(mesh):
    placed = (
        P("band", None, ("comp", "tile")),
        P(None, None, None, ("comp", "tile"), None),
        P(None, None, None, ("comp", "tile")),
        P(),
        P(),
        P(None, None, ("comp", "tile")),
        P(None, ("comp", "tile"), None),
        P(("comp", "tile"), None),
        P(),
        P("band", ("comp", "tile"), None),
        P("band", ("comp", "tile")),
        P(),
        P(),
        P(),
        P(),
        P(),
        P(),
        P(),
        P(None, ("comp", "tile")),
    )
    return jax.shard_map(
        on_device,
        mesh=mesh,
        in_specs=placed,
        out_specs=(
            P("band", None, ("comp", "tile")),
            P("band", ("comp", "tile"), None),
            P("band", ("comp", "tile"), None),
        ),
        check_vma=False,
    )
```

```python
import functools
import math

import jax
import jax.numpy as jnp
import numpy as np
from jax import lax
from jax.experimental import pallas as pl
from jax.experimental.pallas import tpu as pltpu
from jax.sharding import PartitionSpec as P

full_precision = lax.Precision.HIGHEST
eps_norm = 1e-06
shrink_level = 0.01
f32 = jnp.float32
bf16 = jnp.bfloat16
quarter = ("comp", "tile")
vmem_bytes = 56 * 1024 * 1024

tail_log2 = (
    -0.9999930608094244,
    -1.1512017040487785,
    -0.45877096697476855,
    -0.053412112881497276,
    0.008080722210665518,
    -0.0007692214388919801,
    3.309301407796759e-05,
)
tail_end = 6.0


def gelu(x):
    a = jnp.minimum(jnp.abs(x), tail_end)
    power = tail_log2[-1] * a + tail_log2[-2]
    for c in tail_log2[-3::-1]:
        power = power * a + c
    return jnp.maximum(x, 0.0) - a * jnp.exp2(power)


def pick(n, cap):
    for t in range(cap, 0, -16):
        if n % t == 0:
            return t
    return n


def pick_rows(tokens, part):
    rows = tokens // part
    return part * max(n for n in range(1, rows + 1) if rows % n == 0 and n * part <= 384)


def dot(a, b):
    return jnp.dot(a, b, preferred_element_type=f32)


def layer_norm(values, scaling, offset):
    average = jnp.mean(values, axis=-1, keepdims=True)
    squares = jnp.mean(values * values, axis=-1, keepdims=True)
    variance = squares - average * average
    return (values - average) * lax.rsqrt(variance + eps_norm) * scaling + offset


def split3(x, axis):
    high = lax.reduce_precision(x, 8, 7)
    low = x - high
    return high.astype(bf16), lax.reduce_precision(low, 8, 7).astype(bf16)


def product_left(x):
    high, low = split3(x, -1)
    return jnp.concatenate([high, low, high], axis=-1)


def product_right(x):
    high, low = split3(x, 0)
    return jnp.concatenate([high, high, low], axis=0)


def whole(shape):
    return pl.BlockSpec(shape, lambda *_: (0,) * len(shape))


def shift_sum(x, axes):
    for axis in axes:
        n = lax.axis_size(axis)
        mine = x
        for d in range(1, n):
            x = x + lax.ppermute(mine, axis, [(i, (i + d) % n) for i in range(n)])
    return x


def spread(x, index, count):
    mine = lax.broadcasted_iota(jnp.int32, (count,) + (1,) * x.ndim, 0) == index
    return shift_sum(jnp.where(mine, x[None], jnp.zeros((), x.dtype)), ("tile", "comp"))


def gathered(x, axes):
    parts = [x]
    for axis in axes:
        n = lax.axis_size(axis)
        parts = parts + [
            lax.ppermute(part, axis, [(i, (i + d) % n) for i in range(n)])
            for d in range(1, n)
            for part in parts
        ]
    return parts


def gathered_pairs(x, y, axes):
    return gathered(x, axes), gathered(y, axes)


def mlp_rows(filtered, gain, shift, w_in, w_out):
    n2 = layer_norm(filtered, gain, shift).astype(bf16)
    total = filtered
    hidden = dot(n2, w_in[0][...])
    for at, b in enumerate(w_out):
        ready = hidden
        if at + 1 < len(w_in):
            hidden = dot(n2, w_in[at + 1][...])
        total = total + dot(gelu(ready).astype(bf16), b[...])
    return total.astype(bf16)


def first_mlp_kernel(n, u_ref, gain, shift, head, *refs):
    w_in, w_out, (out_ref, flux_ref) = refs[:n], refs[n : 2 * n], refs[2 * n :]
    u = jnp.concatenate([u_ref[i].astype(f32) for i in range(u_ref.shape[0])], axis=-1)
    out = mlp_rows(u, gain[...], shift[...], w_in, w_out)
    out_ref[...] = out
    flux_ref[...] = dot(out, head[...])


def first_mlp(u, gain, shift, head, w_in, w_out):
    slots, tokens, width = u.shape
    full = slots * width
    tile = pick(tokens, 384)
    n = len(w_in)
    hidden = sum(w.shape[1] for w in w_in)
    return pl.pallas_call(
        functools.partial(first_mlp_kernel, n),
        grid=(tokens // tile,),
        in_specs=[
            pl.BlockSpec((slots, tile, width), lambda i: (0, i, 0)),
            whole((1, full)),
            whole((1, full)),
            whole(head.shape),
        ]
        + [whole(w.shape) for w in w_in]
        + [whole(w.shape) for w in w_out],
        out_specs=[
            pl.BlockSpec((tile, full), lambda i: (i, 0)),
            pl.BlockSpec((tile, head.shape[1]), lambda i: (i, 0)),
        ],
        out_shape=[
            jax.ShapeDtypeStruct((tokens, full), bf16),
            jax.ShapeDtypeStruct((tokens, head.shape[1]), f32),
        ],
        compiler_params=pltpu.CompilerParams(vmem_limit_bytes=vmem_bytes),
        cost_estimate=pl.CostEstimate(
            flops=4 * tokens * full * hidden,
            bytes_accessed=4 * tokens * full + 4 * full * hidden,
            transcendentals=tokens * hidden,
        ),
    )(u, gain, shift, head, *w_in, *w_out)


def second_mlp_kernel(n, v_ref, r_ref, gain0, shift0, gain, shift, *refs):
    w_in, w_out, out_ref = refs[:n], refs[n : 2 * n], refs[2 * n]
    v = v_ref[...].astype(f32)
    r = jnp.concatenate([r_ref[i].astype(f32) for i in range(r_ref.shape[0])], axis=-1)
    u = (v + r + layer_norm(v, gain0[...], shift0[...])).astype(bf16).astype(f32)
    out = mlp_rows(u, gain[...], shift[...], w_in, w_out)
    width = out_ref.shape[3]
    for i in range(out_ref.shape[0]):
        out_ref[i] = out[:, i * width : (i + 1) * width].reshape(out_ref.shape[1:])


def second_mlp(v, r, gain0, shift0, gain, shift, w_in, w_out, part):
    slots, tokens, width = r.shape
    full = slots * width
    tile = pick_rows(tokens, part)
    n = len(w_in)
    hidden = sum(w.shape[1] for w in w_in)
    return pl.pallas_call(
        functools.partial(second_mlp_kernel, n),
        grid=(tokens // tile,),
        in_specs=[
            pl.BlockSpec((tile, full), lambda i: (i, 0)),
            pl.BlockSpec((slots, tile, width), lambda i: (0, i, 0)),
        ]
        + [whole((1, full))] * 4
        + [whole(w.shape) for w in w_in]
        + [whole(w.shape) for w in w_out],
        out_specs=pl.BlockSpec((slots, tile // part, part, width), lambda i: (0, i, 0, 0)),
        out_shape=jax.ShapeDtypeStruct((slots, tokens // part, part, width), bf16),
        compiler_params=pltpu.CompilerParams(vmem_limit_bytes=vmem_bytes),
        cost_estimate=pl.CostEstimate(
            flops=4 * tokens * full * hidden,
            bytes_accessed=6 * tokens * full + 4 * full * hidden,
            transcendentals=tokens * hidden,
        ),
    )(v, r, gain0, shift0, gain, shift, *w_in, *w_out)


def middle_kernel(a_ref, p_ref, e_ref, gain, shift, v_ref, n_ref):
    v = (a_ref[...].astype(f32) + dot(p_ref[...], e_ref[...])).astype(bf16)
    v_ref[...] = v
    normed = layer_norm(v.astype(f32), gain[...], shift[...]).astype(bf16)
    width = n_ref.shape[3]
    for i in range(n_ref.shape[0]):
        n_ref[i] = normed[:, i * width : (i + 1) * width].reshape(n_ref.shape[1:])


def make_middle(a, patches, embed, gain, shift, slots, part):
    tokens, full = a.shape
    tile = pick_rows(tokens, part)
    return pl.pallas_call(
        middle_kernel,
        grid=(tokens // tile,),
        in_specs=[
            pl.BlockSpec((tile, full), lambda i: (i, 0)),
            pl.BlockSpec((tile, patches.shape[1]), lambda i: (i, 0)),
            whole(embed.shape),
            whole((1, full)),
            whole((1, full)),
        ],
        out_specs=[
            pl.BlockSpec((tile, full), lambda i: (i, 0)),
            pl.BlockSpec((slots, tile // part, part, full // slots), lambda i: (0, i, 0, 0)),
        ],
        out_shape=[
            jax.ShapeDtypeStruct((tokens, full), bf16),
            jax.ShapeDtypeStruct((slots, tokens // part, part, full // slots), bf16),
        ],
        compiler_params=pltpu.CompilerParams(vmem_limit_bytes=vmem_bytes),
    )(a, patches, embed, gain, shift)


def soft_shrink(y):
    return y - jnp.clip(y, -shrink_level, shrink_level)


def modes_kernel(halves, pair, x_refs, fwd, back, weights, biases, z_refs):
    width = weights.shape[2]
    waves = z_refs[0].shape[0]
    for k in range(waves):
        x = jnp.concatenate(
            [
                x_refs[h][2 * k + part, :, j * width : (j + 1) * width]
                for part in range(2)
                for h in range(halves)
                for j in range(pair)
            ],
            axis=0,
        )
        lats = x.shape[0] // 2
        s = dot(fwd[...], x).astype(bf16)
        for layer in range(2):
            s_re, s_im = s[:lats], s[lats:]
            y_re = dot(s_re, weights[layer, 0]) - dot(s_im, weights[layer, 1])
            y_im = dot(s_im, weights[layer, 0]) + dot(s_re, weights[layer, 1])
            y_re = y_re + biases[layer, 0]
            y_im = y_im + biases[layer, 1]
            if layer == 0:
                y_re, y_im = jnp.maximum(y_re, 0.0), jnp.maximum(y_im, 0.0)
            else:
                y_re, y_im = soft_shrink(y_re), soft_shrink(y_im)
            s = jnp.concatenate([y_re.astype(bf16), y_im.astype(bf16)], axis=0)
        z = dot(back[...], s)
        rows = z.shape[0] // (halves * pair)
        for h in range(halves):
            cut = [z[(h * pair + j) * rows : (h * pair + j + 1) * rows] for j in range(pair)]
            z_refs[h][k] = jnp.concatenate(cut, axis=-1).astype(bf16)


def mix_modes(xs, fwd, back, weights, biases, pair, early):
    halves = len(xs)
    parts, rows, lanes = xs[0].shape
    waves = parts // 2
    lats = fwd.shape[0] // 2
    width = lanes // pair
    step = 3 if waves % 3 == 0 else 1

    def kernel(*refs):
        x_refs, refs = refs[:halves], refs[halves:]
        z_refs = refs[4 + len(early) :]
        modes_kernel(halves, pair, x_refs, *refs[:4], z_refs)

    return pl.pallas_call(
        kernel,
        grid=(waves // step,),
        in_specs=[pl.BlockSpec((2 * step, rows, lanes), lambda i: (i, 0, 0))] * halves
        + [whole(fwd.shape), whole(back.shape), whole(weights.shape), whole(biases.shape)]
        + [pl.BlockSpec(memory_space=pl.ANY)] * len(early),
        out_specs=[pl.BlockSpec((step, 2 * rows, lanes), lambda i: (i, 0, 0))] * halves,
        out_shape=[jax.ShapeDtypeStruct((waves, 2 * rows, lanes), bf16)] * halves,
        compiler_params=pltpu.CompilerParams(vmem_limit_bytes=vmem_bytes),
        cost_estimate=pl.CostEstimate(
            flops=waves * 16 * (lats * lats * width + lats * width * width),
            bytes_accessed=8 * waves * lats * width,
            transcendentals=0,
        ),
    )(*xs, fwd, back, weights, biases, *early)


def norm_with(values, stats, scaling, offset):
    column = jnp.transpose(stats)
    return (values - column[:, 0:1]) * column[:, 1:2] * scaling + offset


def aligned(waves):
    return 2 * waves % 16 == 0


def spectrum_block(bands, waves, lanes):
    if aligned(waves):
        return pl.BlockSpec((bands, 1, 2 * waves, lanes), lambda i: (0, i, 0, 0))
    return pl.BlockSpec((1, bands * 2 * waves, lanes), lambda i: (i, 0, 0))


def lon_forward(source, matrix, bands, waves, pair, stats=None, early=()):
    if stats is None:
        _, rows, part, width = source.shape
    else:
        rows, longitudes, width = source.shape
    lanes = pair * width

    def kernel(*refs):
        x_ref, f_ref, out_ref = refs[0], refs[1], refs[-1]
        columns = []
        for j in range(pair):
            if stats is None:
                columns.append(
                    jnp.concatenate([x_ref[i, j] for i in range(x_ref.shape[0])], axis=0)
                )
            else:
                st_ref, gain, shift = refs[2:5]
                normed = norm_with(x_ref[j].astype(f32), st_ref[j], gain[...], shift[...])
                columns.append(normed.astype(bf16))
        y = dot(f_ref[...], jnp.concatenate(columns, axis=-1)).astype(bf16)
        if aligned(waves):
            out_ref[:, 0] = y.reshape(bands, 2 * waves, lanes)
        else:
            out_ref[0] = y

    if stats is None:
        args = (source, matrix)
        specs = [
            pl.BlockSpec((source.shape[0], pair, part, width), lambda i: (0, i, 0, 0)),
            whole(matrix.shape),
        ]
    else:
        st, gain, shift = stats
        args = (source, matrix, st, gain, shift)
        specs = [
            pl.BlockSpec((pair, longitudes, width), lambda i: (i, 0, 0)),
            whole(matrix.shape),
            pl.BlockSpec((pair, st.shape[1], longitudes), lambda i: (i, 0, 0)),
            whole(gain.shape),
            whole(shift.shape),
        ]
    count = rows // pair
    if aligned(waves):
        shape = (bands, count, 2 * waves, lanes)
    else:
        shape = (count, bands * 2 * waves, lanes)
    out = pl.pallas_call(
        kernel,
        grid=(count,),
        in_specs=specs + [pl.BlockSpec(memory_space=pl.ANY)] * len(early),
        out_specs=spectrum_block(bands, waves, lanes),
        out_shape=jax.ShapeDtypeStruct(shape, bf16),
        compiler_params=pltpu.CompilerParams(vmem_limit_bytes=vmem_bytes),
        cost_estimate=pl.CostEstimate(
            flops=2 * rows * matrix.shape[0] * matrix.shape[1] * width,
            bytes_accessed=4 * rows * matrix.shape[0] * width,
            transcendentals=0,
        ),
    )(*args, *early)
    if not aligned(waves):
        out = out.reshape(count, bands, 2 * waves, lanes).transpose(1, 0, 2, 3)
    return out


def lon_back_call(z, matrix, slots, pair, source=None, stats=None, early=()):
    bands, count, parts, lanes = z.shape
    waves = parts // 2
    width = lanes // pair
    longitudes = matrix.shape[0]
    part = longitudes // slots
    if not aligned(waves):
        z = z.transpose(1, 0, 2, 3).reshape(count, bands * parts, lanes)

    def kernel(*refs):
        z_ref, g_ref, out_ref = refs[0], refs[1], refs[-1]
        spectra = z_ref[:, 0].reshape(bands * parts, lanes) if aligned(waves) else z_ref[0]
        r = dot(g_ref[...], spectra)
        for j in range(pair):
            u = r[:, j * width : (j + 1) * width]
            if stats is not None:
                v_ref, st_ref, gain, shift = refs[2:6]
                v = v_ref[j].astype(f32)
                u = v + u + norm_with(v, st_ref[j], gain[...], shift[...])
            u = u.astype(bf16)
            for i in range(slots):
                out_ref[i, j] = u[i * part : (i + 1) * part]

    args = [z, matrix]
    specs = [spectrum_block(bands, waves, lanes), whole(matrix.shape)]
    if stats is not None:
        st, gain, shift = stats
        args += [source, st, gain, shift]
        specs += [
            pl.BlockSpec((pair, longitudes, width), lambda i: (i, 0, 0)),
            pl.BlockSpec((pair, st.shape[1], longitudes), lambda i: (i, 0, 0)),
            whole(gain.shape),
            whole(shift.shape),
        ]
    return pl.pallas_call(
        kernel,
        grid=(count,),
        in_specs=specs + [pl.BlockSpec(memory_space=pl.ANY)] * len(early),
        out_specs=pl.BlockSpec((slots, pair, part, width), lambda i: (0, i, 0, 0)),
        out_shape=jax.ShapeDtypeStruct((slots, count * pair, part, width), bf16),
        compiler_params=pltpu.CompilerParams(vmem_limit_bytes=vmem_bytes),
        cost_estimate=pl.CostEstimate(
            flops=2 * count * longitudes * bands * parts * lanes,
            bytes_accessed=6 * count * longitudes * lanes,
            transcendentals=0,
        ),
    )(*args, *early)


def assemble_kernel(halves, *refs):
    out_ref = refs[halves]
    rows = refs[0].shape[1]
    for h in range(halves):
        out_ref[h * rows : (h + 1) * rows] = refs[h][0]


def assemble(outs):
    halves = len(outs)
    slots, rows, part, width = outs[0].shape
    return pl.pallas_call(
        functools.partial(assemble_kernel, halves),
        grid=(slots,),
        in_specs=[pl.BlockSpec((1, rows, part, width), lambda i: (i, 0, 0, 0))] * halves,
        out_specs=pl.BlockSpec((halves * rows, part, width), lambda i: (0, i, 0)),
        out_shape=jax.ShapeDtypeStruct((halves * rows, slots * part, width), bf16),
        compiler_params=pltpu.CompilerParams(vmem_limit_bytes=vmem_bytes),
    )(*outs)


def ocean_block(extended, taps, gain, shift, mask, w_in, w_out, scale, head, early):
    lane = 128
    size = taps.shape[0]
    reach = size // 2
    side = -(-reach // 8) * 8
    columns = extended.shape[1] - 2 * side
    rows = extended.shape[0] - 2 * reach
    width = extended.shape[2]
    lane_parts = width // lane
    blocks = 16 // lane_parts
    block = columns // blocks
    span = block + 2 * side
    tile = blocks * lane_parts
    fields = head.shape[1]
    step = max(n for n in range(1, 5) if rows % n == 0)
    group = 4

    taps = taps.reshape(size * size, 1, lane_parts, lane)
    taps = jnp.broadcast_to(taps, (size * size, blocks, lane_parts, lane))
    taps = taps.reshape(size * size, tile, lane).astype(bf16)
    high = lax.reduce_precision(head, 8, 7)
    mid = lax.reduce_precision(head - high, 8, 7)
    heads = jnp.concatenate([high, mid, head - high - mid], axis=1).astype(bf16)

    def kernel(*refs):
        x_ref, t_ref, gain, shift, mask_ref, w_in, w_out, scale, head = refs[:9]
        next_ref, field_ref, laid, held, summed, normed = refs[9 + len(early) :]
        at = pl.program_id(0)

        @pl.when(at == 0)
        def _():
            def lay(r, carry):
                row = x_ref[r].astype(f32)
                for b in range(blocks):
                    for p in range(lane_parts):
                        held[pl.ds(b * lane_parts + p, span, stride=tile), :] = row[
                            b * block : b * block + span, p * lane : (p + 1) * lane
                        ]
                laid[r] = held[...].astype(bf16)
                return carry

            lax.fori_loop(0, rows + 2 * reach, lay, 0)

        def correlate(r, carry):
            for first in range(0, block, group):
                count = min(group, block - first)
                total = [None] * count
                for a in range(size):
                    near = [
                        laid[at * step + r + a, pl.ds((side - reach + first + t) * tile, tile), :]
                        for t in range(count + size - 1)
                    ]
                    for q in range(count):
                        part = near[q] * t_ref[a * size]
                        for e in range(1, size):
                            part = part + near[q + e] * t_ref[a * size + e]
                        part = part.astype(f32)
                        total[q] = part if total[q] is None else total[q] + part
                for q in range(count):
                    summed[pl.ds((first + q) * tile, tile), :] = total[q]
            for b in range(blocks):
                cut = [
                    summed[pl.ds(b * lane_parts + p, block, stride=tile), :]
                    for p in range(lane_parts)
                ]
                cells = jnp.concatenate(cut, axis=-1)
                normed[r, b * block : (b + 1) * block] = layer_norm(cells, gain[...], shift[...])
            return carry

        lax.fori_loop(0, step, correlate, 0)
        cells = normed[...].reshape(step * columns, width).astype(bf16)
        half = w_in.shape[1] // 2
        update = None
        for i in range(2):
            h = gelu(dot(cells, w_in[:, i * half : (i + 1) * half])).astype(bf16)
            part = dot(h, w_out[i * half : (i + 1) * half, :])
            update = part if update is None else update + part
        mask = mask_ref[...]
        first = at * step + reach
        start = x_ref[pl.ds(first, step), side : side + columns, :].astype(f32)
        start = start.reshape(step * columns, width)
        out = (start + mask * (scale[...] * update)).astype(bf16)
        next_ref[...] = out
        parts = dot(out, head[...])
        field_ref[...] = mask * (
            parts[:, :fields] + parts[:, fields : 2 * fields] + parts[:, 2 * fields :]
        )

    cells = rows * columns
    by_cell = lambda n: pl.BlockSpec((step * columns, n), lambda i: (i, 0))
    return pl.pallas_call(
        kernel,
        grid=(rows // step,),
        in_specs=[
            whole(extended.shape),
            whole(taps.shape),
            whole((1, width)),
            whole((1, width)),
            by_cell(1),
            whole(w_in.shape),
            whole(w_out.shape),
            whole((1, width)),
            whole(heads.shape),
        ]
        + [pl.BlockSpec(memory_space=pl.ANY)] * len(early),
        out_specs=[by_cell(width), by_cell(fields)],
        out_shape=[
            jax.ShapeDtypeStruct((cells, width), bf16),
            jax.ShapeDtypeStruct((cells, fields), f32),
        ],
        scratch_shapes=[
            pltpu.VMEM((rows + 2 * reach, span * tile, lane), bf16),
            pltpu.VMEM((span * tile, lane), f32),
            pltpu.VMEM((block * tile, lane), f32),
            pltpu.VMEM((step, columns, width), f32),
        ],
        compiler_params=pltpu.CompilerParams(vmem_limit_bytes=vmem_bytes),
        cost_estimate=pl.CostEstimate(
            flops=4 * cells * width * w_in.shape[1] + 100 * cells * width,
            bytes_accessed=8 * cells * width,
            transcendentals=cells * w_in.shape[1],
        ),
    )(extended, taps, gain[None], shift[None], mask, w_in, w_out, scale[None], heads, *early)


def lon_matrices(longitudes, bands):
    kept = longitudes // 2
    scale = 1.0 / math.sqrt(longitudes)
    turns = np.arange(longitudes)[:, None] * np.arange(kept)[None] % longitudes
    angles = turns * (2.0 * math.pi / longitudes)
    cos, sin = np.cos(angles) * scale, np.sin(angles) * scale
    weight = np.where(np.arange(kept) == 0, 1.0, 2.0)[None]

    def laid(re, im):
        return np.stack([re, im], axis=-1).reshape(longitudes, -1)

    fwd = np.ascontiguousarray(laid(cos, -sin).T)
    back = laid(cos * weight, -sin * weight)
    return jnp.asarray(fwd, bf16), jnp.asarray(back, bf16)


def lat_matrices(lats, bands, halves, pair):
    order = np.arange(lats).reshape(bands, halves, lats // (bands * halves * pair), pair)
    order = order.transpose(1, 3, 0, 2).reshape(1, lats)
    angles = (np.arange(lats)[:, None] * order % lats) * (2.0 * math.pi / lats)
    cos = np.cos(angles) / math.sqrt(lats)
    sin = np.sin(angles) / math.sqrt(lats)
    fwd = np.block([[cos, sin], [-sin, cos]])
    cos_t = cos.T.reshape(halves * pair, -1, lats)
    sin_t = sin.T.reshape(halves * pair, -1, lats)
    back = np.concatenate(
        [np.concatenate([cos_t, -sin_t], axis=2), np.concatenate([sin_t, cos_t], axis=2)], axis=1
    ).reshape(2 * lats, 2 * lats)
    return jnp.asarray(fwd, bf16), jnp.asarray(back, bf16)


def dense_groups(weights):
    width, group = weights.shape[-2], weights.shape[-1]
    groups = width // group
    tiled = jnp.concatenate([weights] * groups, axis=-1)
    row = lax.broadcasted_iota(jnp.int32, (width, width), 0) // group
    column = lax.broadcasted_iota(jnp.int32, (width, width), 1) // group
    return jnp.where(row == column, tiled, 0.0).astype(bf16)


def to_band(x):
    return lax.all_to_all(x, "band", split_axis=0, concat_axis=0, tiled=True)


def to_quarter(x):
    return lax.all_to_all(x, quarter, split_axis=0, concat_axis=0, tiled=True)


def to_quarter_steps(x, index):
    n = x.shape[0]
    take = lambda a, i: lax.dynamic_index_in_dim(a, i % n, 0, keepdims=False)
    parts = [take(x, index)]
    for d in range(1, n):
        pairs = [(i, (i + d) % n) for i in range(n)]
        parts.append(lax.ppermute(take(x, index + d), quarter, pairs))
    here = [take_of(parts, (index - i) % n) for i in range(n)]
    return jnp.stack(here)


def take_of(parts, which):
    out = parts[0]
    for d in range(1, len(parts)):
        out = jnp.where(which == d, parts[d], out)
    return out


def modes_of_bands(xs, fwd, back, weights, biases, pair, early):
    bands, count, parts, lanes = xs[0].shape
    xs = [to_band(x) for x in xs]
    xs = [x.transpose(2, 0, 1, 3).reshape(parts, bands * count, lanes) for x in xs]
    zs = mix_modes(xs, fwd, back, weights, biases, pair, early)
    zs = [z.reshape(parts // 2, 2, bands, count, lanes).transpose(2, 3, 0, 1, 4) for z in zs]
    return [z.reshape(bands, count, parts, lanes) for z in zs]


def with_halo(cells, reach):
    side = -(-reach // 8) * 8
    count = lax.axis_size(quarter)
    right = [(i, (i + 1) % count) for i in range(count)]
    left = [((i + 1) % count, i) for i in range(count)]
    before = lax.ppermute(cells[:, -side:], quarter, right)
    after = lax.ppermute(cells[:, :side], quarter, left)
    wide = lambda r: jnp.concatenate([before[r], cells[r], after[r]], axis=1)
    count = lax.axis_size("band")
    down = [(i, i + 1) for i in range(count - 1)]
    up = [(i + 1, i) for i in range(count - 1)]
    above = lax.ppermute(wide(slice(-reach, None)), "band", down)
    below = lax.ppermute(wide(slice(0, reach)), "band", up)
    return jnp.concatenate([above, wide(slice(None)), below], axis=0)


def on_device(
    atmosphere,
    spec_weight,
    spec_bias,
    norm_gain,
    norm_shift,
    fc_in,
    fc_out,
    flux_head,
    flux_embed,
    ocean_state,
    sea_mask,
    depth_kernel,
    ocean_gain,
    ocean_shift,
    ocean_in,
    ocean_out,
    layer_scale,
    field_head,
    patch_embed,
):
    column_index = lax.axis_index(quarter)
    slots = lax.axis_size(quarter)
    bands = lax.axis_size("band")
    rows, longitudes, slot = atmosphere.shape
    width_full = slot * slots
    part = longitudes // slots
    waves = longitudes // 2 // bands
    halves = 2 if rows % 4 == 0 else 1
    pair = 2 if rows % (2 * halves) == 0 else 1
    half = rows // halves
    lon_fwd, lon_back = lon_matrices(longitudes, bands)
    lat_fwd, lat_back = lat_matrices(rows * bands, bands, halves, pair)
    weights = dense_groups(spec_weight)
    biases = spec_bias[:, :, :, None, :]
    heads = spread(flux_head, column_index, slots).reshape(-1, flux_head.shape[1])
    embed = spread(patch_embed, column_index, slots).transpose(1, 0, 2)
    embed = product_right(embed.reshape(patch_embed.shape[0], -1))
    gain = lambda b, i: norm_gain[b, i][None]
    shift = lambda b, i: norm_shift[b, i][None]
    cut = lambda x, h: lax.slice_in_dim(x, h * half, (h + 1) * half)
    in0, out0 = gathered_pairs(fc_in[0], fc_out[0], ("comp", "tile"))
    in1, out1 = gathered_pairs(fc_in[1], fc_out[1], ("comp", "tile"))

    values = atmosphere.astype(f32)
    sums = jnp.stack([jnp.sum(values, axis=-1), jnp.sum(values * values, axis=-1)])
    sums = shift_sum(sums, ("tile", "comp")) / width_full
    rstd = lax.rsqrt(sums[1] - sums[0] * sums[0] + eps_norm)
    stats = jnp.stack([sums[0], rstd] + [jnp.zeros_like(rstd)] * 6, axis=1)
    scaling = lax.dynamic_slice_in_dim(norm_gain[0, 0], column_index * slot, slot)[None]
    offset = lax.dynamic_slice_in_dim(norm_shift[0, 0], column_index * slot, slot)[None]
    streams = [cut(atmosphere, h) for h in range(halves)]
    stats = [(cut(stats, h), scaling, offset) for h in range(halves)]
    spectra = [
        lon_forward(streams[h], lon_fwd, bands, waves, pair, stats[h]) for h in range(halves)
    ]
    spectra = modes_of_bands(
        spectra, lat_fwd, lat_back, weights[0], biases[0], pair, in0 + out0 + [heads, embed]
    )
    spectra = [to_band(z) for z in spectra]
    after_one, fluxes = [], []
    for h in range(halves):
        u = lon_back_call(
            spectra[h], lon_back, slots, pair, streams[h], stats[h], in1 + out1 if h == 0 else ()
        )
        u = to_quarter_steps(u, column_index) if h + 1 < halves else to_quarter(u)
        u = u.reshape(slots, half * part, slot)
        a, f = first_mlp(u, gain(0, 1), shift(0, 1), heads, in0, out0)
        after_one.append(a)
        fluxes.append(f.reshape(half, part, -1))

    fluxes = jnp.concatenate(fluxes, axis=0)
    upsampled = jnp.repeat(jnp.repeat(fluxes, 2, axis=0), 2, axis=1)
    sea_cells = sea_mask.astype(f32)[..., None]
    forcing = jnp.einsum("ijf,fc->ijc", upsampled, flux_embed, precision=full_precision)
    start = (ocean_state.astype(f32) + sea_cells * forcing).astype(bf16)
    reach = depth_kernel.shape[0] // 2
    extended = with_halo(start, reach)
    tile_columns = start.shape[1]
    pieces = 2 if halves == 2 and half % 2 == 0 else 1
    tile_rows = start.shape[0] // (halves * pieces)
    cells = tile_rows * tile_columns
    nexts, surfaces, middles, spectra, waiting = [], [], [], [], []
    for h in range(halves):
        patches = []
        for piece in range(pieces):
            first = (h * pieces + piece) * tile_rows
            ocean_next, surface = ocean_block(
                extended[first : first + tile_rows + 2 * reach],
                depth_kernel,
                ocean_gain,
                ocean_shift,
                sea_cells[first : first + tile_rows].reshape(cells, 1),
                ocean_in,
                ocean_out,
                layer_scale,
                field_head,
                spectra[:1] if piece == pieces - 1 else [],
            )
            if waiting:
                spectra.append(
                    lon_forward(waiting.pop(), lon_fwd, bands, waves, pair, early=(ocean_next,))
                )
            nexts.append(ocean_next.reshape((tile_rows,) + start.shape[1:]))
            surface = surface.reshape(tile_rows, tile_columns, -1)
            surfaces.append(surface)
            patches.append(
                surface.reshape(tile_rows // 2, 2, part, 2, surface.shape[2])
                .transpose(0, 2, 4, 1, 3)
                .reshape(tile_rows // 2 * part, -1)
            )
        middle, normed = make_middle(
            after_one[h],
            product_left(jnp.concatenate(patches, axis=0)),
            embed,
            gain(1, 0),
            shift(1, 0),
            slots,
            part,
        )
        middles.append(middle)
        waiting.append(to_quarter_steps(normed, column_index))
    spectra.append(lon_forward(waiting.pop(), lon_fwd, bands, waves, pair))
    ocean_next = jnp.concatenate(nexts, axis=0)
    surface = jnp.concatenate(surfaces, axis=0)

    spectra = modes_of_bands(spectra, lat_fwd, lat_back, weights[1], biases[1], pair, [])
    spectra = [to_band(z) for z in spectra]
    outs = []
    for h in range(halves):
        restored = lon_back_call(spectra[h], lon_back, slots, pair)
        last = h + 1 == halves
        restored = to_quarter(restored) if last else to_quarter_steps(restored, column_index)
        restored = restored.reshape(slots, half * part, slot)
        out = second_mlp(
            middles[h], restored, gain(1, 0), shift(1, 0), gain(1, 1), shift(1, 1), in1, out1, part
        )
        outs.append(to_quarter(out))
    return (assemble(outs), ocean_next, surface)


def solution(mesh):
    placed = (
        P("band", None, ("comp", "tile")),
        P(None, None, None, ("comp", "tile"), None),
        P(None, None, None, ("comp", "tile")),
        P(),
        P(),
        P(None, None, ("comp", "tile")),
        P(None, ("comp", "tile"), None),
        P(("comp", "tile"), None),
        P(),
        P("band", ("comp", "tile"), None),
        P("band", ("comp", "tile")),
        P(),
        P(),
        P(),
        P(),
        P(),
        P(),
        P(),
        P(None, ("comp", "tile")),
    )
    return jax.shard_map(
        on_device,
        mesh=mesh,
        in_specs=placed,
        out_specs=(
            P("band", None, ("comp", "tile")),
            P("band", ("comp", "tile"), None),
            P("band", ("comp", "tile"), None),
        ),
        check_vma=False,
    )
```
